512 devices in a mesh: patch: 64 (over z, y_hi, core), head: 8 (over x, y_lo).
Axes of the slice: x: 4, y: 4 (y_hi: 2, y_lo: 2; y = y_hi * 2 + y_lo), z: 16, core: 2. Of those that a mesh axis runs over, the one named last changes fastest.
Arguments:
- hidden_states: bfloat16 [8192, 3072], P('patch', 'head'), may hold values from -500 to 500, as said below
- shift_mod: float32 [3072], replicated, may hold values from -3 to 3
- scale_mod: float32 [3072], replicated, may hold values from -3 to 3
- gate_mod: float32 [3072], P('head'), may hold values from 1 to 6
- qkv_weight: bfloat16 [3072, 3, 2048], P('patch', None, 'head'), may hold values from -0.109375 to 0.109375
- query_gain: float32 [128], replicated, may hold values from 1 to 2.5
- key_gain: float32 [128], replicated, may hold values from 1 to 2.5
- text_keys: bfloat16 [512, 2048], P(None, 'head'), may hold values from -6 to 6
- text_values: bfloat16 [512, 2048], P(None, 'head'), may hold values from -6 to 6
- stale_keys: bfloat16 [8192, 2048], P('patch', 'head'), may hold values from -330 to 330, as said below
- stale_values: bfloat16 [8192, 2048], P('patch', 'head'), may hold values from -6 to 6
- out_weight: bfloat16 [2048, 3072], P('head'), may hold values from -0.125 to 0.125
Outputs:
- update: bfloat16 [8192, 3072], P('patch', 'head')
The draws below stay inside these ranges and needn't reach their ends.
Inputs may be any that keep to these rules, and one draw needn't show every extreme that they name: `hidden_states`: finite real values. `stale_keys`: finite real values.
All inputs are finite; a program needn't handle non-finite values.
Results may differ from the reference program's by a relative error of at most 0.02.
The reference program's roundings to bfloat16 on the way (of `modulated`, `weights` and `attention`) count: a program that leaves them out, or rounds other values in their place, can miss the bound.
Values may be sent and summed in bfloat16 or wider, within the bound.
A program may use at most 64 MiB of HBM per device.

```python
import math
import jax
import jax.numpy as jnp
from jax import lax

D = 3072
HEADS = 16
HD = 128
TXT = 512
TOK_DEV = 128
TOKENS = 8192
N_PATCH = 64


def draw_hidden_states(key, part):
    key = jax.random.fold_in(key, 11)
    base_key, row_key, col_key = jax.random.split(key, 3)
    row_scale = jnp.exp(jax.random.uniform(row_key, (TOKENS, 1), jnp.float32) * math.log(10.0))
    col_scale = jnp.exp(jax.random.uniform(col_key, (1, D), jnp.float32) * math.log(10.0))
    base = jnp.clip(jax.random.normal(base_key, (TOKENS, D), jnp.float32), -4.0, 4.0)
    return (base * row_scale * col_scale).astype(jnp.bfloat16)


def draw_stale_keys(key, part):
    key = jax.random.fold_in(key, 23)
    base_key = jax.random.fold_in(key, 0)
    shape = (TOKENS, HEADS * HD)
    base = jnp.clip(jax.random.normal(base_key, shape, jnp.float32), -4.0, 4.0) * 1.5
    return base.astype(jnp.bfloat16)


def block_scale(own_key, shape, shards, smallest, high):
    factor_of = 1.0
    for dim, parts in shards:
        draws = jax.random.uniform(jax.random.fold_in(jax.random.fold_in(own_key, 6), dim), (parts,), jnp.float32, smallest / len(shards), high / len(shards))
        factor_of = factor_of * jnp.repeat(jnp.exp(draws), shape[dim] // parts).reshape((-1,) + (1,) * (len(shape) - 1 - dim))
    return factor_of


def noise(rng, extent, scale, bound, shards=(), kind=jnp.bfloat16):
    drawn = jax.random.normal(rng, extent, jnp.float32) * scale
    if len(shards) > 0:
        drawn = block_scale(rng, extent, shards, -0.22, 0.18) * drawn
    return jnp.clip(drawn, min=-bound, max=bound).astype(kind)


def setup_inputs(seed: int = 0) -> dict:
    seeds = jax.random.split(jax.random.key(seed), 13)
    return {
        "hidden_states": draw_hidden_states(jax.random.fold_in(seeds[12], 71), 0),
        "shift_mod": noise(seeds[1], (D,), 0.5, 3.0, (), jnp.float32),
        "scale_mod": noise(seeds[2], (D,), 0.5, 3.0, (), jnp.float32),
        "gate_mod": jnp.clip(jnp.exp(math.log(6.0) - 1.7917595 * jax.random.uniform(seeds[3], (D,), jnp.float32) ** block_scale(seeds[3], (D,), ((0, 8),), -0.2, 0.2)), 1.0, 6.0),
        "qkv_weight": noise(seeds[4], (D, 3, HEADS * HD), D ** -0.5, 0.109375, ((0, 64), (2, 8))),
        "query_gain": jnp.clip(jnp.exp(jax.random.uniform(seeds[5], (HD,), jnp.float32, math.log(1.0), math.log(2.5))), 1.0, 2.5),
        "key_gain": jnp.clip(jnp.exp(jax.random.uniform(seeds[6], (HD,), jnp.float32, math.log(1.0), math.log(2.5))), 1.0, 2.5),
        "text_keys": noise(seeds[7], (TXT, HEADS * HD), 1.5, 6.0, ((1, 8),)),
        "text_values": noise(seeds[8], (TXT, HEADS * HD), 1.0, 6.0, ((1, 8),)),
        "stale_keys": draw_stale_keys(jax.random.fold_in(seeds[12], 71), 0),
        "stale_values": noise(seeds[10], (TOKENS, HEADS * HD), 1.0, 6.0, ((0, 64), (1, 8))),
        "out_weight": noise(seeds[11], (HEADS * HD, D), (HEADS * HD) ** -0.5, 0.125, ((0, 8),)),
    }


def head_norm(raw, gain):
    power = lax.optimization_barrier(jnp.mean(raw * raw, axis=-1, keepdims=True))
    return raw * lax.rsqrt(power + 1e-06) * gain

def reference(hidden_states, shift_mod, scale_mod, gate_mod, qkv_weight, query_gain, key_gain, text_keys, text_values, stale_keys, stale_values, out_weight):
    widths = HEADS * HD
    states = hidden_states.astype(jnp.float32)
    center = lax.optimization_barrier(jnp.mean(states, axis=-1, keepdims=True))
    spread = lax.optimization_barrier(jnp.mean((states - center) ** 2, axis=-1, keepdims=True))
    normed = (states - center) * lax.rsqrt(spread + 1e-06)
    modulated = ((1.0 + scale_mod) * normed + shift_mod).astype(jnp.bfloat16)
    projected = jnp.dot(modulated, qkv_weight.reshape(D, 3 * widths), preferred_element_type=jnp.float32)
    projected = projected.reshape(TOKENS, 3, HEADS, HD)
    queries = head_norm(projected[:, 0], query_gain).astype(jnp.bfloat16)
    fresh_keys = head_norm(projected[:, 1], key_gain).astype(jnp.bfloat16).reshape(TOKENS, widths)
    fresh_values = projected[:, 2].astype(jnp.bfloat16).reshape(TOKENS, widths)
    factor = HD ** (-0.5)

    def per_patch(index):
        begin = (index * TOK_DEV).astype(jnp.int32)
        zero = jnp.zeros((), jnp.int32)
        query_block = lax.dynamic_slice_in_dim(queries, begin, TOK_DEV, 0)
        own_keys = lax.dynamic_slice_in_dim(fresh_keys, begin, TOK_DEV, 0)
        own_values = lax.dynamic_slice_in_dim(fresh_values, begin, TOK_DEV, 0)
        image_keys = lax.dynamic_update_slice(stale_keys, own_keys, (begin, zero))
        image_values = lax.dynamic_update_slice(stale_values, own_values, (begin, zero))
        all_keys = jnp.concatenate([text_keys, image_keys], axis=0).reshape(TXT + TOKENS, HEADS, HD)
        all_values = jnp.concatenate([text_values, image_values], axis=0).reshape(TXT + TOKENS, HEADS, HD)
        scores = jnp.einsum('qhd,khd->hqk', query_block.astype(jnp.float32), all_keys.astype(jnp.float32)) * factor
        peak = lax.optimization_barrier(jnp.max(scores, axis=-1, keepdims=True))
        exps = jnp.exp(scores - peak)
        totals = lax.optimization_barrier(jnp.sum(exps, axis=-1))
        weights = exps.astype(jnp.bfloat16).astype(jnp.float32)
        mixed = jnp.einsum('hqk,khd->qhd', weights, all_values.astype(jnp.float32))
        result = mixed / jnp.transpose(totals)[:, :, None]
        return result.astype(jnp.bfloat16).reshape(TOK_DEV, widths)
    attention = lax.map(per_patch, jnp.arange(N_PATCH, dtype=jnp.int32)).reshape(TOKENS, widths)
    summed = jnp.dot(attention, out_weight, preferred_element_type=jnp.float32)
    return (summed * gate_mod).astype(jnp.bfloat16)
```

```python
import functools
import math

import jax
import jax.numpy as jnp
from jax import lax
from jax.experimental import pallas as pl
from jax.experimental.pallas import tpu as pltpu
from jax.sharding import PartitionSpec as P

MESH = pl.DeviceIdType.MESH
NZ = 16
F32 = jnp.float32
BF16 = jnp.bfloat16
COPY = pltpu.make_async_remote_copy
EXP_SCALE = 128 ** (-0.5) * math.log2(math.e)
PEERS = [(dx, dl, dh) for dh in (0, 1) for dl in (0, 1) for dx in range(4)][1:]
OUT_PEERS = [(dx, dl) for dl in (0, 1) for dx in range(4)][1:]


def kernel(
    hidden,
    shift,
    scale,
    gate,
    weight,
    query_gain,
    key_gain,
    text_keys,
    text_values,
    stale_keys,
    stale_values,
    out_weight,
    out,
    hid,
    mod,
    wbuf,
    kv,
    text,
    wo,
    gathered,
    mine,
    own,
    proj,
    queries,
    peak,
    total,
    mixed,
    loc_sem,
    swap_send,
    swap_recv,
    ring_send,
    ring_recv,
    sib_send,
    sib_recv,
    hid_send,
    hid_recv,
    wo_send,
    wo_recv,
    wos_send,
    wos_recv,
    att_send,
    att_recv,
):
    me = lax.axis_index("patch")
    group = lax.axis_index("head")
    z, yh, c = me // 4, lax.rem(me // 2, 2), lax.rem(me, 2)
    x, yl = group // 2, lax.rem(group, 2)
    head = group * 2 + yh
    other_core = (z * 4 + yh * 2 + 1 - c, group)
    next_z = (lax.rem(z + 1, NZ) * 4 + yh * 2 + c, group)
    last_z = (lax.rem(z + NZ - 1, NZ) * 4 + yh * 2 + c, group)
    swap = (z * 4 + (1 - yh) * 2 + c, group)

    def plane_peer(dx, dl, dh):
        there = lax.rem(x + dx, 4) * 2 + lax.rem(yl + dl, 2)
        return (z * 4 + lax.rem(yh + dh, 2) * 2 + c, there)

    barrier = pltpu.get_barrier_semaphore()
    everyone = [other_core, next_z, last_z] + [plane_peer(*d) for d in PEERS]
    for peer in everyone:
        pl.semaphore_signal(barrier, inc=1, device_id=peer, device_id_type=MESH)

    here = pl.ds(pl.multiple_of(yh * 128, 128), 128)
    there = pl.ds(pl.multiple_of((1 - yh) * 128, 128), 128)
    columns = pl.ds(pl.multiple_of(group * 384, 384), 384)
    local = [
        pltpu.make_async_copy(weight.at[yh], wbuf.at[me], loc_sem.at[0]),
        pltpu.make_async_copy(stale_keys.at[:, here], kv.at[me, pl.ds(0, 128)], loc_sem.at[1]),
        pltpu.make_async_copy(stale_values.at[:, here], kv.at[me, pl.ds(128, 128)], loc_sem.at[2]),
        pltpu.make_async_copy(hidden, hid.at[yh, group], loc_sem.at[3]),
        pltpu.make_async_copy(text_keys.at[:, here], text.at[0], loc_sem.at[4]),
        pltpu.make_async_copy(text_values.at[:, here], text.at[1], loc_sem.at[5]),
        pltpu.make_async_copy(out_weight.at[:, columns], wo.at[group], loc_sem.at[6]),
    ]
    for copy in local:
        copy.start()

    pl.semaphore_wait(barrier, len(everyone))

    def chunk(kind, stream, offset, core):
        side = yh if stream == 0 else 1 - yh
        index = lax.rem(z + offset + NZ, NZ) * 4 + side * 2 + core
        return (wbuf if kind == 0 else kv).at[index]

    def ring(kind, stream, way, step):
        ref = chunk(kind, stream, (1 - step) if way == 0 else (step - 1), c)
        at = (kind * 2 + stream) * 2 + way
        return COPY(
            ref, ref, ring_send.at[at, step], ring_recv.at[at, step],
            device_id=next_z if way == 0 else last_z, device_id_type=MESH,
        )

    def ring_arrival(kind, stream, way, step):
        ref = chunk(kind, stream, -step if way == 0 else step, c)
        at = (kind * 2 + stream) * 2 + way
        return COPY(
            ref, ref, ring_send.at[at, step], ring_recv.at[at, step],
            device_id=next_z if way == 0 else last_z, device_id_type=MESH,
        )

    def sibling(kind, stream, offset, core):
        ref = chunk(kind, stream, offset, core)
        at, slot = kind * 2 + stream, lax.rem(offset + NZ, NZ)
        return COPY(
            ref, ref, sib_send.at[at, slot], sib_recv.at[at, slot],
            device_id=other_core, device_id_type=MESH,
        )

    def swap_copy(src, dst, at):
        return COPY(
            src, dst, swap_send.at[at], swap_recv.at[at], device_id=swap, device_id_type=MESH
        )

    swaps = [
        swap_copy(weight.at[1 - yh], wbuf.at[me], 0),
        swap_copy(stale_keys.at[:, there], kv.at[me, pl.ds(0, 128)], 1),
        swap_copy(stale_values.at[:, there], kv.at[me, pl.ds(128, 128)], 2),
    ]
    partner = z * 4 + (1 - yh) * 2 + c
    swap_arrivals = [
        swap_copy(weight.at[1 - yh], wbuf.at[partner], 0),
        swap_copy(stale_keys.at[:, there], kv.at[partner, pl.ds(0, 128)], 1),
        swap_copy(stale_values.at[:, there], kv.at[partner, pl.ds(128, 128)], 2),
    ]

    def hid_copy(at, dx, dl, dh):
        return COPY(
            hidden, hid.at[yh, group], hid_send.at[at], hid_recv.at[at],
            device_id=plane_peer(dx, dl, dh), device_id_type=MESH,
        )

    def source_group(dx, dl):
        return lax.rem(x + 4 - dx, 4) * 2 + lax.rem(yl + dl, 2)

    def hid_arrival(at, dx, dl, dh):
        slot = hid.at[lax.rem(yh + dh, 2), source_group(dx, dl)]
        return COPY(
            slot, slot, hid_send.at[at], hid_recv.at[at],
            device_id=plane_peer(dx, dl, dh), device_id_type=MESH,
        )

    half = pl.ds(pl.multiple_of(c * 128, 128), 128)
    other_half = pl.ds(pl.multiple_of((1 - c) * 128, 128), 128)

    def wo_copy(at, dx, dl):
        peer = plane_peer(dx, dl, 0)
        src = out_weight.at[half, pl.ds(pl.multiple_of(peer[1] * 384, 384), 384)]
        return COPY(
            src, wo.at[group, half], wo_send.at[at], wo_recv.at[at],
            device_id=peer, device_id_type=MESH,
        )

    def wo_arrival(at, dx, dl):
        slot = wo.at[source_group(dx, dl), half]
        return COPY(
            slot, slot, wo_send.at[at], wo_recv.at[at],
            device_id=plane_peer(dx, dl, 0), device_id_type=MESH,
        )

    def wo_share(at, dx, dl, rows):
        slot = wo.at[source_group(dx, dl), rows]
        return COPY(
            slot, slot, wos_send.at[at], wos_recv.at[at],
            device_id=other_core, device_id_type=MESH,
        )

    swaps[0].start()
    local[0].wait()
    ring(0, 0, 0, 1).start()
    ring(0, 0, 1, 1).start()
    swaps[1].start()
    swaps[2].start()
    sibling(0, 0, 0, c).start()
    local[1].wait()
    local[2].wait()
    ring(1, 0, 0, 1).start()
    ring(1, 0, 1, 1).start()
    sibling(1, 0, 0, c).start()
    for at, d in enumerate(PEERS):
        hid_copy(at, *d).start()
    swap_arrivals[0].wait_recv()
    ring(0, 1, 0, 1).start()
    ring(0, 1, 1, 1).start()
    sibling(0, 1, 0, c).start()
    swap_arrivals[1].wait_recv()
    swap_arrivals[2].wait_recv()
    ring(1, 1, 0, 1).start()
    ring(1, 1, 1, 1).start()
    sibling(1, 1, 0, c).start()
    for at, d in enumerate(OUT_PEERS):
        wo_copy(at, *d).start()

    def forward(kind, step):
        for stream in (0, 1):
            for way in (0, 1):
                ring_arrival(kind, stream, way, step).wait_recv()
                ring(kind, stream, way, step + 1).start()
                sibling(kind, stream, -step if way == 0 else step, c).start()

    def forward_seventh(kind):
        for stream in (0, 1):
            for way in (0, 1):
                ring_arrival(kind, stream, way, 7).wait_recv()
                if stream == way:
                    ring(kind, stream, way, 8).start()
                sibling(kind, stream, -7 if way == 0 else 7, c).start()

    def forward_eighth(kind):
        for way in (0, 1):
            ring_arrival(kind, way, way, 8).wait_recv()
            sibling(kind, way, 8, c).start()

    @pl.loop(1, 7)
    def _(step):
        forward(0, step)

    forward_seventh(0)
    forward(1, 1)
    forward_eighth(0)
    forward(1, 2)

    def norm(side):
        @pl.loop(0, 8)
        def _(block):
            rows = pl.ds(pl.multiple_of(block * 16, 16), 16)
            states = jnp.concatenate([hid[side, g, rows, :] for g in range(8)], axis=1)
            states = states.astype(F32)
            center = jnp.mean(states, axis=-1, keepdims=True)
            states = states - center
            spread = jnp.mean(states * states, axis=-1, keepdims=True)
            normed = states * lax.rsqrt(spread + 1e-06)
            modulated = (1.0 + scale[...]) * normed + shift[...]
            there = pl.ds(pl.multiple_of(side * 128 + block * 16, 16), 16)
            mod[there, :] = modulated.astype(BF16)

    local[3].wait()
    for at, d in enumerate(PEERS):
        hid_arrival(at, *d).wait_recv()
    norm(0)
    forward(1, 3)
    norm(1)

    @pl.loop(0, NZ)
    def _(slot):
        sibling(0, 0, slot, 1 - c).wait_recv()
        sibling(0, 1, slot, 1 - c).wait_recv()

    proj[...] = jnp.zeros_like(proj)

    @pl.loop(0, 8)
    def _(part):
        features = pl.ds(pl.multiple_of(part * 384, 384), 384)
        rows = wbuf[pl.ds(part * 8, 8)].reshape(384, 384)
        proj[...] += jnp.dot(mod[:, features], rows, preferred_element_type=F32)

    forward(1, 4)

    def head_norm(raw, gain):
        power = jnp.mean(raw * raw, axis=-1, keepdims=True)
        return (raw * lax.rsqrt(power + 1e-06) * gain).astype(BF16)

    queries[...] = head_norm(proj[:, 0:128], query_gain[...])

    def scores_of(rows, keys):
        return lax.dot_general(
            queries[rows, :], keys, (((1,), (1,)), ((), ())), preferred_element_type=F32
        )

    def lane_sums(exps):
        parts = [exps[:, i : i + 128] for i in range(0, exps.shape[1], 128)]
        return functools.reduce(lambda a, b: a + b, parts)

    def start_attend(rows, keys, values):
        scores = scores_of(rows, keys)
        top = jnp.max(scores, axis=-1, keepdims=True)
        exps = jnp.exp2((scores - top) * EXP_SCALE)
        peak[rows, :] = jnp.broadcast_to(top, (scores.shape[0], 128))
        total[rows, :] = lane_sums(exps)
        mixed[rows, :] = jnp.dot(exps.astype(BF16), values, preferred_element_type=F32)

    def attend(rows, keys, values):
        scores = scores_of(rows, keys)
        before = peak[rows, :]
        top = jnp.maximum(before, jnp.max(scores, axis=-1, keepdims=True))
        rescale = jnp.exp2((before - top) * EXP_SCALE)
        exps = jnp.exp2((scores - top[:, 0:1]) * EXP_SCALE)
        peak[rows, :] = top
        total[rows, :] = total[rows, :] * rescale + lane_sums(exps)
        mixed[rows, :] = mixed[rows, :] * rescale + jnp.dot(
            exps.astype(BF16), values, preferred_element_type=F32
        )

    every = pl.ds(0, 256)
    local[4].wait()
    local[5].wait()
    start_attend(every, text[0], text[1])

    sibling(1, 0, 0, 1 - c).wait_recv()
    sibling(1, 1, 0, 1 - c).wait_recv()
    for side in (0, 1):
        rows = pl.ds(side * 128, 128)
        own[...] = kv[pl.ds(z * 4, 4)]
        own[side * 2 + c, 0:128, :] = head_norm(proj[rows, 128:256], key_gain[...])
        own[side * 2 + c, 128:256, :] = proj[rows, 256:384].astype(BF16)
        attend(rows, own[:, 0:128, :].reshape(512, 128), own[:, 128:256, :].reshape(512, 128))

    def attend_plane(offset):
        sibling(1, 0, offset, 1 - c).wait_recv()
        sibling(1, 1, offset, 1 - c).wait_recv()
        base = lax.rem(z + offset + NZ, NZ) * 4
        keys = kv[pl.ds(base, 4), 0:128, :].reshape(512, 128)
        values = kv[pl.ds(base, 4), 128:256, :].reshape(512, 128)
        attend(every, keys, values)

    def attend_pairs(first, count):
        @pl.loop(0, 2 * count)
        def _(i):
            distance = first + i // 2
            attend_plane(lax.rem(i, 2) * (NZ - 2 * distance) + distance)

    forward(1, 5)
    attend_pairs(1, 2)
    forward(1, 6)
    for at, d in enumerate(OUT_PEERS):
        wo_arrival(at, *d).wait_recv()
        wo_share(at, *d, half).start()
    attend_pairs(3, 2)
    forward_seventh(1)
    attend_pairs(5, 2)
    forward_eighth(1)
    attend_pairs(7, 1)
    attend_plane(8)

    attention = (mixed[...] / jnp.sum(total[...], axis=-1, keepdims=True)).astype(BF16)
    mine[0] = attention[0:128]
    mine[1] = attention[128:256]
    gathered[head] = mine[yh]

    def att_copy(at, dx, dl, dh):
        return COPY(
            mine.at[lax.rem(yh + dh, 2)], gathered.at[head], att_send.at[at], att_recv.at[at],
            device_id=plane_peer(dx, dl, dh), device_id_type=MESH,
        )

    def att_arrival(at, dx, dl, dh):
        slot = gathered.at[source_group(dx, dl) * 2 + lax.rem(yh + dh, 2)]
        return COPY(
            slot, slot, att_send.at[at], att_recv.at[at],
            device_id=plane_peer(dx, dl, dh), device_id_type=MESH,
        )

    for at, d in enumerate(PEERS):
        att_copy(at, *d).start()
    local[6].wait()
    for at, d in enumerate(OUT_PEERS):
        wo_share(at, *d, other_half).wait_recv()
    for at, d in enumerate(PEERS):
        att_arrival(at, *d).wait_recv()
    summed = jnp.zeros((128, 384), F32)
    for g in range(8):
        left = jnp.concatenate([gathered[2 * g], gathered[2 * g + 1]], axis=1)
        summed += jnp.dot(left, wo[g], preferred_element_type=F32)
    out[...] = (summed * gate[...]).astype(BF16)

    for copy in swaps:
        copy.wait_send()
    for at, d in enumerate(PEERS):
        hid_copy(at, *d).wait_send()
        att_copy(at, *d).wait_send()
    for at, d in enumerate(OUT_PEERS):
        wo_copy(at, *d).wait_send()
        wo_share(at, *d, half).wait_send()
    for kind in (0, 1):
        for stream in (0, 1):
            for way in (0, 1):
                @pl.loop(1, 8)
                def _(step):
                    ring(kind, stream, way, step).wait_send()
            ring(kind, stream, stream, 8).wait_send()

            @pl.loop(0, NZ)
            def _(slot):
                sibling(kind, stream, slot, c).wait_send()


def per_device(
    hidden_states,
    shift_mod,
    scale_mod,
    gate_mod,
    qkv_weight,
    query_gain,
    key_gain,
    text_keys,
    text_values,
    stale_keys,
    stale_values,
    out_weight,
):
    weight = qkv_weight.reshape(48, 3, 2, 128).transpose(2, 0, 1, 3).reshape(2, 48, 384)
    dma = pltpu.SemaphoreType.DMA
    vmem = pl.BlockSpec(memory_space=pltpu.VMEM)
    hbm = pl.BlockSpec(memory_space=pl.ANY)
    n, m = len(PEERS), len(OUT_PEERS)
    return pl.pallas_call(
        kernel,
        name="joint_attention",
        out_shape=jax.ShapeDtypeStruct((128, 384), BF16),
        in_specs=[hbm, vmem, vmem, vmem, hbm, vmem, vmem, hbm, hbm, hbm, hbm, hbm],
        out_specs=vmem,
        scratch_shapes=[
            pltpu.VMEM((2, 8, 128, 384), BF16),
            pltpu.VMEM((256, 3072), BF16),
            pltpu.VMEM((64, 48, 384), BF16),
            pltpu.VMEM((64, 256, 128), BF16),
            pltpu.VMEM((2, 512, 128), BF16),
            pltpu.VMEM((8, 256, 384), BF16),
            pltpu.VMEM((16, 128, 128), BF16),
            pltpu.VMEM((2, 128, 128), BF16),
            pltpu.VMEM((4, 256, 128), BF16),
            pltpu.VMEM((256, 384), F32),
            pltpu.VMEM((256, 128), BF16),
            pltpu.VMEM((256, 128), F32),
            pltpu.VMEM((256, 128), F32),
            pltpu.VMEM((256, 128), F32),
            dma((7,)),
            dma((3,)),
            dma((3,)),
            dma((8, 9)),
            dma((8, 9)),
            dma((4, NZ)),
            dma((4, NZ)),
            dma((n,)),
            dma((n,)),
            dma((m,)),
            dma((m,)),
            dma((m,)),
            dma((m,)),
            dma((n,)),
            dma((n,)),
        ],
        compiler_params=pltpu.CompilerParams(
            collective_id=0, has_side_effects=True, vmem_limit_bytes=48 * 1024 * 1024
        ),
        cost_estimate=pl.CostEstimate(
            flops=2_200_000_000, bytes_accessed=16_000_000, transcendentals=2_300_000
        ),
    )(
        hidden_states,
        shift_mod.reshape(1, -1),
        scale_mod.reshape(1, -1),
        gate_mod.reshape(1, -1),
        weight,
        query_gain.reshape(1, -1),
        key_gain.reshape(1, -1),
        text_keys,
        text_values,
        stale_keys,
        stale_values,
        out_weight,
    )


def solution(mesh):
    placed = (
        P("patch", "head"),
        P(),
        P(),
        P("head"),
        P("patch", None, "head"),
        P(),
        P(),
        P(None, "head"),
        P(None, "head"),
        P("patch", "head"),
        P("patch", "head"),
        P("head", None),
    )
    return jax.shard_map(
        per_device, mesh=mesh, in_specs=placed, out_specs=P("patch", "head"), check_vma=False
    )
```

```python
import functools

import math

import jax
import jax.numpy as jnp
from jax import lax
from jax.experimental import pallas as pl
from jax.experimental.pallas import tpu as pltpu
from jax.sharding import PartitionSpec as P

MESH = pl.DeviceIdType.MESH
ORDER = (
    ("W", 0, 1), ("K", 0, 1), ("W", 1, 0), ("V", 0, 1), ("K", 1, 0), ("W", 0, 2), ("V", 1, 0), ("W", 1, 1),
    ("K", 0, 2), ("W", 0, 3), ("V", 0, 2), ("W", 1, 2), ("K", 1, 1), ("V", 1, 1), ("W", 0, 4), ("K", 0, 3),
    ("W", 1, 3), ("V", 0, 3), ("K", 1, 2), ("W", 0, 5), ("V", 1, 2), ("W", 1, 4), ("K", 0, 4), ("V", 0, 4),
    ("W", 0, 6), ("K", 1, 3), ("W", 1, 5), ("V", 1, 3), ("N", 0, 0), ("K", 0, 5), ("N", 1, 0), ("W", 0, 7),
    ("N", 2, 0), ("V", 0, 5), ("N", 3, 0), ("K", 1, 4), ("W", 1, 6), ("V", 1, 4), ("W", 0, 8), ("K", 0, 6),
    ("V", 0, 6), ("K", 1, 5), ("W", 1, 7), ("V", 1, 5), ("K", 0, 7), ("V", 0, 7), ("K", 1, 6), ("W", 1, 8),
    ("V", 1, 6), ("K", 0, 8), ("P", 0, 0), ("V", 0, 8), ("K", 1, 7), ("O", 0, 0), ("S", 0, 0), ("V", 1, 7),
    ("A", 1, 2), ("K", 1, 8), ("A", 3, 1), ("V", 1, 8), ("A", 4, 4), ("L", 0, 0),
)
WEIGHTS, KEYS, VALUES = "WKV"
KINDS = (WEIGHTS, KEYS, VALUES)

NZ = 16
F32 = jnp.float32
BF16 = jnp.bfloat16
COPY = pltpu.make_async_remote_copy
EXP_SCALE = 128 ** (-0.5) * math.log2(math.e)
PEERS = [(dx, dl, dh) for dh in (0, 1) for dl in (0, 1) for dx in range(4)][1:]
OUT_PEERS = [(dx, dl) for dl in (0, 1) for dx in range(4)][1:]


def kernel(
    hidden,
    shift,
    scale,
    gate,
    weight,
    query_gain,
    key_gain,
    text_keys,
    text_values,
    stale_keys,
    stale_values,
    out_weight,
    out,
    hid,
    mod,
    wbuf,
    kbuf,
    vbuf,
    shift_row,
    scale_row,
    gate_row,
    gains,
    text,
    wo,
    gathered,
    mine,
    own_keys,
    own_values,
    proj,
    queries,
    peak,
    total,
    mixed,
    loc_sem,
    swap_send,
    swap_recv,
    ring_send,
    ring_recv,
    sib_send,
    sib_recv,
    hid_send,
    hid_recv,
    wo_send,
    wo_recv,
    wos_send,
    wos_recv,
    att_send,
    att_recv,
):
    me = lax.axis_index("patch")
    group = lax.axis_index("head")
    z, yh, c = me // 4, lax.rem(me // 2, 2), lax.rem(me, 2)
    x, yl = group // 2, lax.rem(group, 2)
    head = group * 2 + yh
    other_core = (z * 4 + yh * 2 + 1 - c, group)
    next_z = (lax.rem(z + 1, NZ) * 4 + yh * 2 + c, group)
    last_z = (lax.rem(z + NZ - 1, NZ) * 4 + yh * 2 + c, group)
    swap = (z * 4 + (1 - yh) * 2 + c, group)

    def plane_peer(dx, dl, dh):
        there = lax.rem(x + dx, 4) * 2 + lax.rem(yl + dl, 2)
        return (z * 4 + lax.rem(yh + dh, 2) * 2 + c, there)

    barrier = pltpu.get_barrier_semaphore()
    everyone = [other_core, next_z, last_z] + [plane_peer(*d) for d in PEERS]
    for peer in everyone:
        pl.semaphore_signal(barrier, inc=1, device_id=peer, device_id_type=MESH)

    here = pl.ds(pl.multiple_of(yh * 128, 128), 128)
    there = pl.ds(pl.multiple_of((1 - yh) * 128, 128), 128)
    columns = pl.ds(pl.multiple_of(group * 384, 384), 384)
    local = {
        KEYS: pltpu.make_async_copy(stale_keys.at[:, here], kbuf.at[me], loc_sem.at[0]),
        VALUES: pltpu.make_async_copy(stale_values.at[:, here], vbuf.at[me], loc_sem.at[1]),
        "hidden": pltpu.make_async_copy(hidden, hid.at[yh, group], loc_sem.at[2]),
        "shift": pltpu.make_async_copy(shift, shift_row, loc_sem.at[3]),
        "scale": pltpu.make_async_copy(scale, scale_row, loc_sem.at[4]),
        "text_keys": pltpu.make_async_copy(text_keys.at[:, here], text.at[0], loc_sem.at[5]),
        "text_values": pltpu.make_async_copy(text_values.at[:, here], text.at[1], loc_sem.at[6]),
        "query_gain": pltpu.make_async_copy(query_gain, gains.at[0], loc_sem.at[7]),
        "key_gain": pltpu.make_async_copy(key_gain, gains.at[1], loc_sem.at[8]),
        "gate": pltpu.make_async_copy(gate, gate_row, loc_sem.at[9]),
        "out_weight": pltpu.make_async_copy(
            out_weight.at[:, columns], wo.at[group], loc_sem.at[10]
        ),
    }
    for part in range(3):
        local[part] = pltpu.make_async_copy(
            weight.at[part, :, here],
            wbuf.at[me, :, pl.ds(part * 128, 128)],
            loc_sem.at[11 + part],
        )
    for name in (0, 1, 2, KEYS, VALUES):
        local[name].start()
    for name, copy in local.items():
        if name not in (0, 1, 2, KEYS, VALUES):
            copy.start()

    pl.semaphore_wait(barrier, len(everyone))

    def chunk(kind, stream, offset, core):
        side = yh if stream == 0 else 1 - yh
        index = lax.rem(z + offset + NZ, NZ) * 4 + side * 2 + core
        return {WEIGHTS: wbuf, KEYS: kbuf, VALUES: vbuf}[kind].at[index]

    def ring(kind, stream, way, step):
        ref = chunk(kind, stream, (1 - step) if way == 0 else (step - 1), c)
        at = (KINDS.index(kind) * 2 + stream) * 2 + way
        return COPY(
            ref, ref, ring_send.at[at, step], ring_recv.at[at, step],
            device_id=next_z if way == 0 else last_z, device_id_type=MESH,
        )

    def ring_arrival(kind, stream, way, step):
        ref = chunk(kind, stream, -step if way == 0 else step, c)
        at = (KINDS.index(kind) * 2 + stream) * 2 + way
        return COPY(
            ref, ref, ring_send.at[at, step], ring_recv.at[at, step],
            device_id=next_z if way == 0 else last_z, device_id_type=MESH,
        )

    def sibling(kind, stream, offset, core):
        ref = chunk(kind, stream, offset, core)
        at, slot = KINDS.index(kind) * 2 + stream, lax.rem(offset + NZ, NZ)
        return COPY(
            ref, ref, sib_send.at[at, slot], sib_recv.at[at, slot],
            device_id=other_core, device_id_type=MESH,
        )

    def swap_copy(src, dst, at):
        return COPY(
            src, dst, swap_send.at[at], swap_recv.at[at], device_id=swap, device_id_type=MESH
        )

    partner = z * 4 + (1 - yh) * 2 + c
    swaps = [
        swap_copy(stale_keys.at[:, there], kbuf.at[me], 0),
        swap_copy(stale_values.at[:, there], vbuf.at[me], 1),
    ]
    swaps += [
        swap_copy(weight.at[part, :, there], wbuf.at[me, :, pl.ds(part * 128, 128)], 2 + part)
        for part in range(3)
    ]
    swap_arrivals = [
        swap_copy(kbuf.at[partner], kbuf.at[partner], 0),
        swap_copy(vbuf.at[partner], vbuf.at[partner], 1),
    ]
    for part in range(3):
        slot = wbuf.at[partner, :, pl.ds(part * 128, 128)]
        swap_arrivals.append(swap_copy(slot, slot, 2 + part))

    def hid_copy(at, dx, dl, dh):
        return COPY(
            hidden, hid.at[yh, group], hid_send.at[at], hid_recv.at[at],
            device_id=plane_peer(dx, dl, dh), device_id_type=MESH,
        )

    def source_group(dx, dl):
        return lax.rem(x + 4 - dx, 4) * 2 + lax.rem(yl + dl, 2)

    def hid_arrival(at, dx, dl, dh):
        slot = hid.at[lax.rem(yh + dh, 2), source_group(dx, dl)]
        return COPY(
            slot, slot, hid_send.at[at], hid_recv.at[at],
            device_id=plane_peer(dx, dl, dh), device_id_type=MESH,
        )

    half = pl.ds(pl.multiple_of(c * 128, 128), 128)
    other_half = pl.ds(pl.multiple_of((1 - c) * 128, 128), 128)

    def wo_copy(at, dx, dl):
        peer = plane_peer(dx, dl, 0)
        src = out_weight.at[half, pl.ds(pl.multiple_of(peer[1] * 384, 384), 384)]
        return COPY(
            src, wo.at[group, half], wo_send.at[at], wo_recv.at[at],
            device_id=peer, device_id_type=MESH,
        )

    def wo_arrival(at, dx, dl):
        slot = wo.at[source_group(dx, dl), half]
        return COPY(
            slot, slot, wo_send.at[at], wo_recv.at[at],
            device_id=plane_peer(dx, dl, 0), device_id_type=MESH,
        )

    def wo_share(at, dx, dl, rows):
        slot = wo.at[source_group(dx, dl), rows]
        return COPY(
            slot, slot, wos_send.at[at], wos_recv.at[at],
            device_id=other_core, device_id_type=MESH,
        )

    def forward(kind, stream, step):
        if step == 0:
            if stream == 1:
                at = KINDS.index(kind)
                for copy in swap_arrivals[2:] if at == 0 else swap_arrivals[at - 1 : at]:
                    copy.wait_recv()
            else:
                for name in (0, 1, 2) if kind == WEIGHTS else (kind,):
                    local[name].wait()
            ring(kind, stream, 0, 1).start()
            ring(kind, stream, 1, 1).start()
            sibling(kind, stream, 0, c).start()
            return
        for way in (0, 1):
            if step < 8 or stream == way:
                ring_arrival(kind, stream, way, step).wait_recv()
                if step < 7 or step == 7 and stream == way:
                    ring(kind, stream, way, step + 1).start()
                sibling(kind, stream, -step if way == 0 else step, c).start()

    def norm(part):
        side, begin = part // 2, part % 2 * 4

        @pl.loop(begin, begin + 4, unroll=2)
        def _(block):
            rows = pl.ds(pl.multiple_of(block * 16, 16), 16)
            states = jnp.concatenate([hid[side, g, rows, :] for g in range(8)], axis=1)
            states = states.astype(F32)
            center = jnp.mean(states, axis=-1, keepdims=True)
            states = states - center
            spread = jnp.mean(states * states, axis=-1, keepdims=True)
            normed = states * lax.rsqrt(spread + 1e-06)
            modulated = (1.0 + scale_row[...]) * normed + shift_row[...]
            there = pl.ds(pl.multiple_of(side * 128 + block * 16, 16), 16)
            mod[there, :] = modulated.astype(BF16)

    def arrive_hidden():
        for name in ("hidden", "shift", "scale"):
            local[name].wait()
        for at, d in enumerate(PEERS):
            hid_arrival(at, *d).wait_recv()
        for at, d in enumerate(OUT_PEERS):
            wo_copy(at, *d).start()

    def project():
        @pl.loop(0, NZ)
        def _(slot):
            sibling(WEIGHTS, 0, slot, 1 - c).wait_recv()
            sibling(WEIGHTS, 1, slot, 1 - c).wait_recv()

        proj[...] = jnp.dot(mod[...], wbuf[...].reshape(3072, 384), preferred_element_type=F32)
        for name in ("text_keys", "text_values", "query_gain", "key_gain"):
            local[name].wait()
        queries[...] = head_norm(proj[:, 0:128], gains[0])

    def head_norm(raw, gain):
        power = jnp.mean(raw * raw, axis=-1, keepdims=True)
        return (raw * lax.rsqrt(power + 1e-06) * gain).astype(BF16)


    def scores_of(rows, keys):
        return lax.dot_general(
            queries[rows, :], keys, (((1,), (1,)), ((), ())), preferred_element_type=F32
        )

    def lane_sums(exps):
        parts = [exps[:, i : i + 128] for i in range(0, exps.shape[1], 128)]
        return functools.reduce(lambda a, b: a + b, parts)

    def start_attend(rows, keys, values):
        scores = scores_of(rows, keys)
        top = jnp.max(scores, axis=-1, keepdims=True)
        exps = jnp.exp2((scores - top) * EXP_SCALE)
        peak[rows, :] = jnp.broadcast_to(top, (scores.shape[0], 128))
        total[rows, :] = lane_sums(exps)
        mixed[rows, :] = jnp.dot(exps.astype(BF16), values, preferred_element_type=F32)

    def attend(rows, keys, values):
        scores = scores_of(rows, keys)
        before = peak[rows, :]
        top = jnp.maximum(before, jnp.max(scores, axis=-1, keepdims=True))
        rescale = jnp.exp2((before - top) * EXP_SCALE)
        exps = jnp.exp2((scores - top[:, 0:1]) * EXP_SCALE)
        peak[rows, :] = top
        total[rows, :] = total[rows, :] * rescale + lane_sums(exps)
        mixed[rows, :] = mixed[rows, :] * rescale + jnp.dot(
            exps.astype(BF16), values, preferred_element_type=F32
        )

    every = pl.ds(0, 256)

    def siblings_of(offset):
        for kind in (KEYS, VALUES):
            for stream in (0, 1):
                sibling(kind, stream, offset, 1 - c).wait_recv()

    def attend_own():
        start_attend(every, text[0], text[1])
        siblings_of(0)
        for side in (0, 1):
            rows = pl.ds(side * 128, 128)
            own_keys[...] = kbuf[pl.ds(z * 4, 4)]
            own_values[...] = vbuf[pl.ds(z * 4, 4)]
            own_keys[side * 2 + c] = head_norm(proj[rows, 128:256], gains[1])
            own_values[side * 2 + c] = proj[rows, 256:384].astype(BF16)
            attend(rows, own_keys[...].reshape(512, 128), own_values[...].reshape(512, 128))

    def plane(buf, offset):
        return buf[pl.ds(lax.rem(z + offset, NZ) * 4, 4)].reshape(512, 128)

    def attend_pairs(first, count):
        @pl.loop(first, first + count)
        def _(distance):
            offsets = (distance, NZ - distance)
            for offset in offsets:
                siblings_of(offset)
            keys = jnp.concatenate([plane(kbuf, offset) for offset in offsets], axis=0)
            values = jnp.concatenate([plane(vbuf, offset) for offset in offsets], axis=0)
            attend(every, keys, values)

    def attend_last():
        siblings_of(8)
        attend(every, plane(kbuf, 8), plane(vbuf, 8))

    def share():
        for at, d in enumerate(OUT_PEERS):
            wo_arrival(at, *d).wait_recv()
            wo_share(at, *d, half).start()

    for copy in swaps[2:]:
        copy.start()
    forward(WEIGHTS, 0, 0)
    for copy in swaps[:2]:
        copy.start()
    forward(KEYS, 0, 0)
    forward(VALUES, 0, 0)

    hidden_due = list(enumerate(PEERS))
    for task, first, second in ORDER:
        if hidden_due:
            at, d = hidden_due.pop()
            hid_copy(at, *d).start()
        if task in KINDS:
            forward(task, first, second)
        elif task == "N":
            if first == 0:
                arrive_hidden()
            norm(first)
        elif task == "P":
            project()
        elif task == "O":
            attend_own()
        elif task == "S":
            share()
        elif task == "A":
            attend_pairs(first, second)
        else:
            attend_last()

    def attention(side):
        rows = pl.ds(side * 128, 128)
        sums = jnp.sum(total[rows, :], axis=-1, keepdims=True)
        return (mixed[rows, :] / sums).astype(BF16)

    def att_copy(at, dx, dl, dh):
        return COPY(
            mine.at[lax.rem(yh + dh, 2)], gathered.at[head], att_send.at[at], att_recv.at[at],
            device_id=plane_peer(dx, dl, dh), device_id_type=MESH,
        )

    def att_arrival(at, dx, dl, dh):
        slot = gathered.at[source_group(dx, dl) * 2 + lax.rem(yh + dh, 2)]
        return COPY(
            slot, slot, att_send.at[at], att_recv.at[at],
            device_id=plane_peer(dx, dl, dh), device_id_type=MESH,
        )

    def send_attention(dh):
        side = lax.rem(yh + dh, 2)
        mine[side] = attention(side)
        for at, d in reversed(list(enumerate(PEERS))):
            if d[2] == dh:
                att_copy(at, *d).start()

    send_attention(1)
    send_attention(0)
    gathered[head] = mine[yh]
    local["out_weight"].wait()
    local["gate"].wait()
    for at, d in enumerate(OUT_PEERS):
        wo_share(at, *d, other_half).wait_recv()
    for at, d in enumerate(PEERS):
        att_arrival(at, *d).wait_recv()
    summed = jnp.zeros((128, 384), F32)
    for g in range(8):
        left = jnp.concatenate([gathered[2 * g], gathered[2 * g + 1]], axis=1)
        summed += jnp.dot(left, wo[g], preferred_element_type=F32)
    out[...] = (summed * gate_row[...].reshape(1, 384)).astype(BF16)

    for copy in swaps:
        copy.wait_send()
    for at, d in enumerate(PEERS):
        hid_copy(at, *d).wait_send()
        att_copy(at, *d).wait_send()
    for at, d in enumerate(OUT_PEERS):
        wo_copy(at, *d).wait_send()
        wo_share(at, *d, half).wait_send()
    for kind in KINDS:
        for stream in (0, 1):
            for way in (0, 1):
                @pl.loop(1, 8)
                def _(step):
                    ring(kind, stream, way, step).wait_send()
            ring(kind, stream, stream, 8).wait_send()

            @pl.loop(0, NZ)
            def _(slot):
                sibling(kind, stream, slot, c).wait_send()


def per_device(
    hidden_states,
    shift_mod,
    scale_mod,
    gate_mod,
    qkv_weight,
    query_gain,
    key_gain,
    text_keys,
    text_values,
    stale_keys,
    stale_values,
    out_weight,
):
    dma = pltpu.SemaphoreType.DMA
    vmem = pl.BlockSpec(memory_space=pltpu.VMEM)
    hbm = pl.BlockSpec(memory_space=pltpu.HBM)
    n, m = len(PEERS), len(OUT_PEERS)
    return pl.pallas_call(
        kernel,
        name="joint_attention",
        out_shape=jax.ShapeDtypeStruct((128, 384), BF16),
        in_specs=[hbm] * 12,
        out_specs=vmem,
        scratch_shapes=[
            pltpu.VMEM((2, 8, 128, 384), BF16),
            pltpu.VMEM((256, 3072), BF16),
            pltpu.VMEM((64, 48, 384), BF16),
            pltpu.VMEM((64, 128, 128), BF16),
            pltpu.VMEM((64, 128, 128), BF16),
            pltpu.VMEM((1, 3072), F32),
            pltpu.VMEM((1, 3072), F32),
            pltpu.VMEM((384,), F32),
            pltpu.VMEM((2, 1, 128), F32),
            pltpu.VMEM((2, 512, 128), BF16),
            pltpu.VMEM((8, 256, 384), BF16),
            pltpu.VMEM((16, 128, 128), BF16),
            pltpu.VMEM((2, 128, 128), BF16),
            pltpu.VMEM((4, 128, 128), BF16),
            pltpu.VMEM((4, 128, 128), BF16),
            pltpu.VMEM((256, 384), F32),
            pltpu.VMEM((256, 128), BF16),
            pltpu.VMEM((256, 128), F32),
            pltpu.VMEM((256, 128), F32),
            pltpu.VMEM((256, 128), F32),
            dma((14,)),
            dma((5,)),
            dma((5,)),
            dma((12, 9)),
            dma((12, 9)),
            dma((6, NZ)),
            dma((6, NZ)),
            dma((n,)),
            dma((n,)),
            dma((m,)),
            dma((m,)),
            dma((m,)),
            dma((m,)),
            dma((n,)),
            dma((n,)),
        ],
        compiler_params=pltpu.CompilerParams(
            collective_id=0, has_side_effects=True, vmem_limit_bytes=60 * 1024 * 1024
        ),
        cost_estimate=pl.CostEstimate(
            flops=2_200_000_000, bytes_accessed=16_000_000, transcendentals=2_300_000
        ),
    )(
        hidden_states,
        shift_mod.reshape(1, -1),
        scale_mod.reshape(1, -1),
        gate_mod,
        qkv_weight.transpose(1, 0, 2),
        query_gain.reshape(1, -1),
        key_gain.reshape(1, -1),
        text_keys,
        text_values,
        stale_keys,
        stale_values,
        out_weight,
    )


def solution(mesh):
    placed = (
        P("patch", "head"),
        P(),
        P(),
        P("head"),
        P("patch", None, "head"),
        P(),
        P(),
        P(None, "head"),
        P(None, "head"),
        P("patch", "head"),
        P("patch", "head"),
        P("head", None),
    )
    return jax.shard_map(
        per_device, mesh=mesh, in_specs=placed, out_specs=P("patch", "head"), check_vma=False
    )
```

```python
import functools

import math

import jax
import jax.numpy as jnp
from jax import lax
from jax.experimental import pallas as pl
from jax.experimental.pallas import tpu as pltpu
from jax.sharding import PartitionSpec as P

MESH = pl.DeviceIdType.MESH
ORDER = (
    ("W", 0, 1), ("K", 0, 1), ("W", 1, 0), ("V", 0, 1), ("K", 1, 0), ("W", 0, 2), ("V", 1, 0), ("W", 1, 1),
    ("K", 0, 2), ("W", 0, 3), ("K", 1, 1), ("W", 1, 2), ("V", 1, 1), ("V", 0, 2), ("W", 0, 4), ("K", 1, 2),
    ("W", 1, 3), ("V", 1, 2), ("K", 0, 3), ("W", 0, 5), ("V", 0, 3), ("W", 1, 4), ("K", 1, 3), ("V", 1, 3),
    ("W", 0, 6), ("K", 0, 4), ("W", 1, 5), ("V", 0, 4), ("K", 1, 4), ("N", 0, 0), ("W", 0, 7), ("N", 1, 0),
    ("V", 1, 4), ("N", 2, 0), ("W", 1, 6), ("N", 3, 0), ("Q", 0, 0), ("K", 0, 5), ("V", 0, 5), ("W", 0, 8), ("K", 1, 5),
    ("V", 1, 5), ("W", 1, 7), ("K", 0, 6), ("V", 0, 6), ("K", 1, 6), ("V", 1, 6), ("W", 1, 8), ("K", 0, 7),
    ("P", 0, 0), ("V", 0, 7), ("K", 1, 7), ("V", 1, 7), ("O", 0, 0), ("K", 0, 8), ("A", 1, 2), ("S", 0, 0),
    ("V", 0, 8), ("K", 1, 8), ("V", 1, 8), ("A", 3, 4), ("L", 0, 0),
)
WEIGHTS, KEYS, VALUES = "WKV"
KINDS = (WEIGHTS, KEYS, VALUES)

NZ = 16
F32 = jnp.float32
BF16 = jnp.bfloat16
COPY = pltpu.make_async_remote_copy
EXP_SCALE = 128 ** (-0.5) * math.log2(math.e)
PEERS = [(dx, dl, dh) for dh in (0, 1) for dl in (0, 1) for dx in range(4)][1:]
OUT_PEERS = [(dx, dl) for dl in (0, 1) for dx in range(4)][1:]


def kernel(
    hidden,
    shift,
    scale,
    gate,
    weight,
    query_gain,
    key_gain,
    text_keys,
    text_values,
    stale_keys,
    stale_values,
    out_weight,
    out,
    hid,
    mod,
    stage,
    stage_kv,
    wbuf,
    kv,
    shift_row,
    scale_row,
    gate_row,
    gains,
    text,
    wo,
    gathered,
    mine,
    own_keys,
    own_values,
    proj,
    queries,
    peak,
    total,
    mixed,
    loc_sem,
    swap_send,
    swap_recv,
    ring_send,
    ring_recv,
    sib_send,
    sib_recv,
    hid_send,
    hid_recv,
    wo_send,
    wo_recv,
    wos_send,
    wos_recv,
    att_send,
    att_recv,
):
    me = lax.axis_index("patch")
    group = lax.axis_index("head")
    z, yh, c = me // 4, lax.rem(me // 2, 2), lax.rem(me, 2)
    x, yl = group // 2, lax.rem(group, 2)
    head = group * 2 + yh
    other_core = (z * 4 + yh * 2 + 1 - c, group)
    next_z = (lax.rem(z + 1, NZ) * 4 + yh * 2 + c, group)
    last_z = (lax.rem(z + NZ - 1, NZ) * 4 + yh * 2 + c, group)
    swap = (z * 4 + (1 - yh) * 2 + c, group)

    def plane_peer(dx, dl, dh):
        there = lax.rem(x + dx, 4) * 2 + lax.rem(yl + dl, 2)
        return (z * 4 + lax.rem(yh + dh, 2) * 2 + c, there)

    barrier = pltpu.get_barrier_semaphore()
    everyone = [plane_peer(*d) for d in PEERS[::-1]] + [next_z, last_z, other_core]
    for peer in everyone:
        pl.semaphore_signal(barrier, inc=1, device_id=peer, device_id_type=MESH)

    here = pl.ds(pl.multiple_of(yh * 128, 128), 128)
    there = pl.ds(pl.multiple_of((1 - yh) * 128, 128), 128)
    columns = pl.ds(pl.multiple_of(group * 384, 384), 384)
    local = {
        KEYS: pltpu.make_async_copy(stale_keys.at[:, here], kv.at[me, 0], loc_sem.at[0]),
        VALUES: pltpu.make_async_copy(stale_values.at[:, here], kv.at[me, 1], loc_sem.at[1]),
        "hidden": pltpu.make_async_copy(hidden, hid.at[yh, group], loc_sem.at[2]),
        "shift": pltpu.make_async_copy(shift, shift_row, loc_sem.at[3]),
        "scale": pltpu.make_async_copy(scale, scale_row, loc_sem.at[4]),
        "text_keys": pltpu.make_async_copy(text_keys.at[:, here], text.at[0], loc_sem.at[5]),
        "text_values": pltpu.make_async_copy(text_values.at[:, here], text.at[1], loc_sem.at[6]),
        "query_gain": pltpu.make_async_copy(query_gain, gains.at[0], loc_sem.at[7]),
        "key_gain": pltpu.make_async_copy(key_gain, gains.at[1], loc_sem.at[8]),
        "gate": pltpu.make_async_copy(gate, gate_row, loc_sem.at[9]),
        "out_weight": pltpu.make_async_copy(
            out_weight.at[:, columns], wo.at[group], loc_sem.at[10]
        ),
    }
    local[WEIGHTS] = pltpu.make_async_copy(weight.at[:, :, here], wbuf.at[me], loc_sem.at[11])
    staged = {
        WEIGHTS: pltpu.make_async_copy(weight.at[:, :, there], stage, loc_sem.at[12]),
        KEYS: pltpu.make_async_copy(stale_keys.at[:, there], stage_kv.at[0], loc_sem.at[13]),
        VALUES: pltpu.make_async_copy(stale_values.at[:, there], stage_kv.at[1], loc_sem.at[14]),
    }
    for name in KINDS:
        local[name].start()
        staged[name].start()
    for name, copy in local.items():
        if name not in KINDS:
            copy.start()

    for copy in staged.values():
        copy.wait()
    pl.semaphore_wait(barrier, len(everyone))

    def chunk(kind, stream, offset, core):
        side = yh if stream == 0 else 1 - yh
        index = lax.rem(z + offset + NZ, NZ) * 4 + side * 2 + core
        return wbuf.at[index] if kind == WEIGHTS else kv.at[index, KINDS.index(kind) - 1]

    def ring(kind, stream, way, step):
        ref = chunk(kind, stream, (1 - step) if way == 0 else (step - 1), c)
        at = (KINDS.index(kind) * 2 + stream) * 2 + way
        return COPY(
            ref, ref, ring_send.at[at, step], ring_recv.at[at, step],
            device_id=next_z if way == 0 else last_z, device_id_type=MESH,
        )

    def ring_arrival(kind, stream, way, step):
        ref = chunk(kind, stream, -step if way == 0 else step, c)
        at = (KINDS.index(kind) * 2 + stream) * 2 + way
        return COPY(
            ref, ref, ring_send.at[at, step], ring_recv.at[at, step],
            device_id=next_z if way == 0 else last_z, device_id_type=MESH,
        )

    def sibling(kind, stream, offset, core):
        side = yh if stream == 0 else 1 - yh
        slot = lax.rem(offset + NZ, NZ)
        index = lax.rem(z + slot, NZ) * 4 + side * 2 + core
        ref = wbuf.at[index] if kind == WEIGHTS else kv.at[index]
        at = (kind == VALUES) * 2 + stream
        return COPY(
            ref, ref, sib_send.at[at, slot], sib_recv.at[at, slot],
            device_id=other_core, device_id_type=MESH,
        )

    def swap_copy(src, dst, at):
        return COPY(
            src, dst, swap_send.at[at], swap_recv.at[at], device_id=swap, device_id_type=MESH
        )

    partner = z * 4 + (1 - yh) * 2 + c
    swaps = [
        swap_copy(stage, wbuf.at[me], 0),
        swap_copy(stage_kv.at[0], kv.at[me, 0], 1),
        swap_copy(stage_kv.at[1], kv.at[me, 1], 2),
    ]
    swap_arrivals = [
        swap_copy(wbuf.at[partner], wbuf.at[partner], 0),
        swap_copy(kv.at[partner, 0], kv.at[partner, 0], 1),
        swap_copy(kv.at[partner, 1], kv.at[partner, 1], 2),
    ]

    def hid_copy(at, dx, dl, dh):
        return COPY(
            hidden, hid.at[yh, group], hid_send.at[at], hid_recv.at[at],
            device_id=plane_peer(dx, dl, dh), device_id_type=MESH,
        )

    def source_group(dx, dl):
        return lax.rem(x + 4 - dx, 4) * 2 + lax.rem(yl + dl, 2)

    def hid_arrival(at, dx, dl, dh):
        slot = hid.at[lax.rem(yh + dh, 2), source_group(dx, dl)]
        return COPY(
            slot, slot, hid_send.at[at], hid_recv.at[at],
            device_id=plane_peer(dx, dl, dh), device_id_type=MESH,
        )

    half = pl.ds(pl.multiple_of(c * 128, 128), 128)
    other_half = pl.ds(pl.multiple_of((1 - c) * 128, 128), 128)

    def wo_copy(at, dx, dl):
        peer = plane_peer(dx, dl, 0)
        src = out_weight.at[half, pl.ds(pl.multiple_of(peer[1] * 384, 384), 384)]
        return COPY(
            src, wo.at[group, half], wo_send.at[at], wo_recv.at[at],
            device_id=peer, device_id_type=MESH,
        )

    def wo_arrival(at, dx, dl):
        slot = wo.at[source_group(dx, dl), half]
        return COPY(
            slot, slot, wo_send.at[at], wo_recv.at[at],
            device_id=plane_peer(dx, dl, 0), device_id_type=MESH,
        )

    def wo_share(at, dx, dl, rows):
        slot = wo.at[source_group(dx, dl), rows]
        return COPY(
            slot, slot, wos_send.at[at], wos_recv.at[at],
            device_id=other_core, device_id_type=MESH,
        )

    def forward(kind, stream, step):
        if kind == WEIGHTS and step > 0:
            for offset in {1 - step, step - 1}:
                sibling(kind, stream, offset, 1 - c).wait_recv()
        if step == 0:
            (swap_arrivals[KINDS.index(kind)].wait_recv if stream else local[kind].wait)()
            ring(kind, stream, 0, 1).start()
            ring(kind, stream, 1, 1).start()
            if kind != KEYS:
                sibling(kind, stream, 0, c).start()
            return
        ways = [way for way in (0, 1) if step < 8 or stream == way]
        for way in ways:
            ring_arrival(kind, stream, way, step).wait_recv()
            if step < 7 or step == 7 and stream == way:
                ring(kind, stream, way, step + 1).start()
        for way in ways if kind != KEYS else ():
            sibling(kind, stream, -step if way == 0 else step, c).start()

    def norm(part):
        side, begin = part // 2, part % 2 * 4

        @pl.loop(begin, begin + 4, unroll=2)
        def _(block):
            rows = pl.ds(pl.multiple_of(block * 16, 16), 16)
            states = jnp.concatenate([hid[side, g, rows, :] for g in range(8)], axis=1)
            states = states.astype(F32)
            center = jnp.mean(states, axis=-1, keepdims=True)
            states = states - center
            spread = jnp.mean(states * states, axis=-1, keepdims=True)
            normed = states * lax.rsqrt(spread + 1e-06)
            modulated = (1.0 + scale_row[...]) * normed + shift_row[...]
            there = pl.ds(pl.multiple_of(side * 128 + block * 16, 16), 16)
            mod[there, :] = modulated.astype(BF16)

    def arrive_hidden():
        for name in ("hidden", "shift", "scale"):
            local[name].wait()
        for at, d in enumerate(PEERS):
            hid_arrival(at, *d).wait_recv()
        for at, d in enumerate(OUT_PEERS):
            wo_copy(at, *d).start()

    def project(pairs):
        for pair in pairs:
            at = lax.rem(z // 2 + pair + 8, 8)
            rows = [wbuf[pl.ds(at * 8, 8), part].reshape(384, 128) for part in range(3)]
            features = mod[:, pl.ds(pl.multiple_of(at * 384, 384), 384)]
            term = jnp.dot(features, jnp.concatenate(rows, axis=1), preferred_element_type=F32)
            proj[...] = term if pair == 0 else proj[...] + term

    def finish_projection():
        for stream in (0, 1):
            sibling(WEIGHTS, stream, 8, 1 - c).wait_recv()
        project((-3, 3, 4))
        for name in ("text_keys", "text_values", "query_gain", "key_gain"):
            local[name].wait()
        queries[...] = head_norm(proj[:, 0:128], gains[0])

    def head_norm(raw, gain):
        power = jnp.mean(raw * raw, axis=-1, keepdims=True)
        return (raw * lax.rsqrt(power + 1e-06) * gain).astype(BF16)


    def scores_of(rows, keys):
        return lax.dot_general(
            queries[rows, :], keys, (((1,), (1,)), ((), ())), preferred_element_type=F32
        )

    def lane_sums(exps):
        parts = [exps[:, i : i + 128] for i in range(0, exps.shape[1], 128)]
        return functools.reduce(lambda a, b: a + b, parts)

    def start_attend(rows, keys, values):
        scores = scores_of(rows, keys)
        top = jnp.max(scores, axis=-1, keepdims=True)
        exps = jnp.exp2((scores - top) * EXP_SCALE)
        peak[rows, :] = jnp.broadcast_to(top, (scores.shape[0], 128))
        total[rows, :] = lane_sums(exps)
        mixed[rows, :] = jnp.dot(exps.astype(BF16), values, preferred_element_type=F32)

    def attend(rows, keys, values):
        scores = scores_of(rows, keys)
        before = peak[rows, :]
        top = jnp.maximum(before, jnp.max(scores, axis=-1, keepdims=True))
        rescale = jnp.exp2((before - top) * EXP_SCALE)
        exps = jnp.exp2((scores - top[:, 0:1]) * EXP_SCALE)
        peak[rows, :] = top
        total[rows, :] = total[rows, :] * rescale + lane_sums(exps)
        mixed[rows, :] = mixed[rows, :] * rescale + jnp.dot(
            exps.astype(BF16), values, preferred_element_type=F32
        )

    every = pl.ds(0, 256)

    def siblings_of(offset):
        for stream in (0, 1):
            sibling(VALUES, stream, offset, 1 - c).wait_recv()

    def attend_own():
        start_attend(every, text[0], text[1])
        siblings_of(0)
        for side in (0, 1):
            rows = pl.ds(side * 128, 128)
            own_keys[...] = kv[pl.ds(z * 4, 4), 0]
            own_values[...] = kv[pl.ds(z * 4, 4), 1]
            own_keys[side * 2 + c] = head_norm(proj[rows, 128:256], gains[1])
            own_values[side * 2 + c] = proj[rows, 256:384].astype(BF16)
            attend(rows, own_keys[...].reshape(512, 128), own_values[...].reshape(512, 128))

    def plane(which, offset):
        return kv[pl.ds(lax.rem(z + offset, NZ) * 4, 4), which].reshape(512, 128)

    def attend_planes(offsets):
        for offset in offsets:
            siblings_of(offset)
        keys = jnp.concatenate([plane(0, offset) for offset in offsets], axis=0)
        values = jnp.concatenate([plane(1, offset) for offset in offsets], axis=0)
        attend(every, keys, values)

    def attend_pairs(first, count):
        @pl.loop(0, count // 2)
        def _(i):
            near = first + 2 * i
            attend_planes((near, NZ - near, near + 1, NZ - 1 - near))

    def attend_last():
        attend_planes((7, NZ - 7, 8))

    def share():
        for at, d in enumerate(OUT_PEERS):
            wo_arrival(at, *d).wait_recv()
            wo_share(at, *d, half).start()

    swaps[0].start()
    forward(WEIGHTS, 0, 0)
    swaps[1].start()
    swaps[2].start()
    forward(KEYS, 0, 0)
    forward(VALUES, 0, 0)

    hidden_due = list(enumerate(PEERS))
    for task, first, second in ORDER:
        if hidden_due:
            at, d = hidden_due.pop()
            hid_copy(at, *d).start()
        if task in KINDS:
            forward(task, first, second)
        elif task == "N":
            if first == 0:
                arrive_hidden()
            norm(first)
        elif task == "Q":
            project((0, -1, 1, -2, 2))
        elif task == "P":
            finish_projection()
        elif task == "O":
            attend_own()
        elif task == "S":
            share()
        elif task == "A":
            attend_pairs(first, second)
        else:
            attend_last()

    def attention(side):
        rows = pl.ds(side * 128, 128)
        sums = jnp.sum(total[rows, :], axis=-1, keepdims=True)
        return (mixed[rows, :] / sums).astype(BF16)

    def att_copy(at, dx, dl, dh):
        return COPY(
            mine.at[lax.rem(yh + dh, 2)], gathered.at[head], att_send.at[at], att_recv.at[at],
            device_id=plane_peer(dx, dl, dh), device_id_type=MESH,
        )

    def att_arrival(at, dx, dl, dh):
        slot = gathered.at[source_group(dx, dl) * 2 + lax.rem(yh + dh, 2)]
        return COPY(
            slot, slot, att_send.at[at], att_recv.at[at],
            device_id=plane_peer(dx, dl, dh), device_id_type=MESH,
        )

    def send_attention(dh):
        side = lax.rem(yh + dh, 2)
        mine[side] = attention(side)
        for at, d in reversed(list(enumerate(PEERS))):
            if d[2] == dh:
                att_copy(at, *d).start()

    send_attention(1)
    send_attention(0)

    for copy in swaps:
        copy.wait_send()
    for at, d in enumerate(PEERS):
        hid_copy(at, *d).wait_send()
    for at, d in enumerate(OUT_PEERS):
        wo_copy(at, *d).wait_send()
        wo_share(at, *d, half).wait_send()
    for kind in KINDS:
        for stream in (0, 1):
            for way in (0, 1):

                @pl.loop(1, 8)
                def _(step):
                    ring(kind, stream, way, step).wait_send()

            ring(kind, stream, stream, 8).wait_send()

            @pl.loop(0, NZ if kind != KEYS else 0)
            def _(slot):
                sibling(kind, stream, slot, c).wait_send()

    gathered[head] = mine[yh]
    local["out_weight"].wait()
    local["gate"].wait()
    for at, d in enumerate(OUT_PEERS):
        wo_share(at, *d, other_half).wait_recv()
    for at, d in enumerate(PEERS):
        att_arrival(at, *d).wait_recv()
    summed = jnp.zeros((128, 384), F32)
    for g in range(8):
        left = jnp.concatenate([gathered[2 * g], gathered[2 * g + 1]], axis=1)
        summed += jnp.dot(left, wo[g], preferred_element_type=F32)
    out[...] = (summed * gate_row[...].reshape(1, 384)).astype(BF16)

    for at, d in enumerate(PEERS):
        att_copy(at, *d).wait_send()


def per_device(
    hidden_states,
    shift_mod,
    scale_mod,
    gate_mod,
    qkv_weight,
    query_gain,
    key_gain,
    text_keys,
    text_values,
    stale_keys,
    stale_values,
    out_weight,
):
    dma = pltpu.SemaphoreType.DMA
    vmem = pl.BlockSpec(memory_space=pltpu.VMEM)
    hbm = pl.BlockSpec(memory_space=pltpu.HBM)
    n, m = len(PEERS), len(OUT_PEERS)
    return pl.pallas_call(
        kernel,
        name="joint_attention",
        out_shape=jax.ShapeDtypeStruct((128, 384), BF16),
        in_specs=[hbm] * 12,
        out_specs=vmem,
        scratch_shapes=[
            pltpu.VMEM((2, 8, 128, 384), BF16),
            pltpu.VMEM((256, 3072), BF16),
            pltpu.VMEM((3, 48, 128), BF16),
            pltpu.VMEM((2, 128, 128), BF16),
            pltpu.VMEM((64, 3, 48, 128), BF16),
            pltpu.VMEM((64, 2, 128, 128), BF16),
            pltpu.VMEM((1, 3072), F32),
            pltpu.VMEM((1, 3072), F32),
            pltpu.VMEM((384,), F32),
            pltpu.VMEM((2, 1, 128), F32),
            pltpu.VMEM((2, 512, 128), BF16),
            pltpu.VMEM((8, 256, 384), BF16),
            pltpu.VMEM((16, 128, 128), BF16),
            pltpu.VMEM((2, 128, 128), BF16),
            pltpu.VMEM((4, 128, 128), BF16),
            pltpu.VMEM((4, 128, 128), BF16),
            pltpu.VMEM((256, 384), F32),
            pltpu.VMEM((256, 128), BF16),
            pltpu.VMEM((256, 128), F32),
            pltpu.VMEM((256, 128), F32),
            pltpu.VMEM((256, 128), F32),
            dma((15,)),
            dma((5,)),
            dma((5,)),
            dma((12, 9)),
            dma((12, 9)),
            dma((4, NZ)),
            dma((4, NZ)),
            dma((n,)),
            dma((n,)),
            dma((m,)),
            dma((m,)),
            dma((m,)),
            dma((m,)),
            dma((n,)),
            dma((n,)),
        ],
        compiler_params=pltpu.CompilerParams(
            collective_id=0, has_side_effects=True, vmem_limit_bytes=60 * 1024 * 1024
        ),
        cost_estimate=pl.CostEstimate(
            flops=2_200_000_000, bytes_accessed=16_000_000, transcendentals=2_300_000
        ),
    )(
        hidden_states,
        shift_mod.reshape(1, -1),
        scale_mod.reshape(1, -1),
        gate_mod,
        qkv_weight.transpose(1, 0, 2),
        query_gain.reshape(1, -1),
        key_gain.reshape(1, -1),
        text_keys,
        text_values,
        stale_keys,
        stale_values,
        out_weight,
    )


def solution(mesh):
    placed = (
        P("patch", "head"),
        P(),
        P(),
        P("head"),
        P("patch", None, "head"),
        P(),
        P(),
        P(None, "head"),
        P(None, "head"),
        P("patch", "head"),
        P("patch", "head"),
        P("head", None),
    )
    return jax.shard_map(
        per_device, mesh=mesh, in_specs=placed, out_specs=P("patch", "head"), check_vma=False
    )
```

```python
import functools

import math

import jax
import jax.numpy as jnp
from jax import lax
from jax.experimental import pallas as pl
from jax.experimental.pallas import tpu as pltpu
from jax.sharding import PartitionSpec as P

MESH = pl.DeviceIdType.MESH
ORDER = (
    ("W", 0, 1), ("K", 0, 1), ("W", 1, 0), ("V", 0, 1), ("K", 1, 0), ("W", 0, 2), ("V", 1, 0), ("W", 1, 1),
    ("K", 0, 2), ("W", 0, 3), ("K", 1, 1), ("V", 1, 1), ("W", 1, 2), ("V", 0, 2), ("W", 0, 4), ("K", 1, 2),
    ("W", 1, 3), ("V", 1, 2), ("K", 0, 3), ("W", 0, 5), ("V", 0, 3), ("W", 1, 4), ("K", 1, 3), ("V", 1, 3),
    ("W", 0, 6), ("K", 0, 4), ("W", 1, 5), ("V", 0, 4), ("K", 1, 4), ("W", 0, 7), ("N", 0, 0), ("V", 1, 4),
    ("N", 1, 0), ("K", 0, 5), ("N", 2, 0), ("W", 1, 6), ("N", 3, 0), ("Q", 0, 0), ("V", 0, 5), ("W", 0, 8),
    ("K", 1, 5), ("V", 1, 5), ("K", 0, 6), ("W", 1, 7), ("V", 0, 6), ("K", 1, 6), ("V", 1, 6), ("K", 0, 7),
    ("W", 1, 8), ("V", 0, 7), ("P", 0, 0), ("K", 1, 7), ("V", 1, 7), ("O", 0, 0), ("K", 0, 8), ("A", 1, 2),
    ("S", 0, 0), ("V", 0, 8), ("K", 1, 8), ("V", 1, 8), ("A", 3, 4), ("L", 0, 0),
)
WEIGHTS, KEYS, VALUES = "WKV"
KINDS = (WEIGHTS, KEYS, VALUES)

NZ = 16
F32 = jnp.float32
BF16 = jnp.bfloat16
COPY = pltpu.make_async_remote_copy
EXP_SCALE = 128 ** (-0.5) * math.log2(math.e)
PEERS = [(dx, dl, dh) for dh in (0, 1) for dl in (0, 1) for dx in range(4)][1:]
OUT_PEERS = [(dx, dl) for dl in (0, 1) for dx in range(4)][1:]


def kernel(
    hidden,
    shift,
    scale,
    gate,
    weight,
    query_gain,
    key_gain,
    text_keys,
    text_values,
    stale_keys,
    stale_values,
    out_weight,
    out,
    hid,
    mod,
    stage,
    stage_kv,
    wbuf,
    kv,
    shift_row,
    scale_row,
    gate_row,
    gains,
    text,
    wo,
    gathered,
    mine,
    own_keys,
    own_values,
    proj,
    queries,
    peak,
    total,
    mixed,
    loc_sem,
    swap_send,
    swap_recv,
    ring_send,
    ring_recv,
    sib_send,
    sib_recv,
    hid_send,
    hid_recv,
    wo_send,
    wo_recv,
    wos_send,
    wos_recv,
    att_send,
    att_recv,
):
    me = lax.axis_index("patch")
    group = lax.axis_index("head")
    z, yh, c = me // 4, lax.rem(me // 2, 2), lax.rem(me, 2)
    x, yl = group // 2, lax.rem(group, 2)
    head = group * 2 + yh
    other_core = (z * 4 + yh * 2 + 1 - c, group)
    next_z = (lax.rem(z + 1, NZ) * 4 + yh * 2 + c, group)
    last_z = (lax.rem(z + NZ - 1, NZ) * 4 + yh * 2 + c, group)
    swap = (z * 4 + (1 - yh) * 2 + c, group)

    def plane_peer(dx, dl, dh):
        there = lax.rem(x + dx, 4) * 2 + lax.rem(yl + dl, 2)
        return (z * 4 + lax.rem(yh + dh, 2) * 2 + c, there)

    barrier = pltpu.get_barrier_semaphore()
    everyone = [plane_peer(*d) for d in PEERS[::-1]] + [next_z, last_z, other_core]
    for peer in everyone:
        pl.semaphore_signal(barrier, inc=1, device_id=peer, device_id_type=MESH)

    here = pl.ds(pl.multiple_of(yh * 128, 128), 128)
    there = pl.ds(pl.multiple_of((1 - yh) * 128, 128), 128)
    columns = pl.ds(pl.multiple_of(group * 384, 384), 384)
    local = {
        KEYS: pltpu.make_async_copy(stale_keys.at[:, here], kv.at[me, 0], loc_sem.at[0]),
        VALUES: pltpu.make_async_copy(stale_values.at[:, here], kv.at[me, 1], loc_sem.at[1]),
        "hidden": pltpu.make_async_copy(hidden, hid.at[yh, group], loc_sem.at[2]),
        "shift": pltpu.make_async_copy(shift, shift_row, loc_sem.at[3]),
        "scale": pltpu.make_async_copy(scale, scale_row, loc_sem.at[4]),
        "text_keys": pltpu.make_async_copy(text_keys.at[:, here], text.at[0], loc_sem.at[5]),
        "text_values": pltpu.make_async_copy(text_values.at[:, here], text.at[1], loc_sem.at[6]),
        "query_gain": pltpu.make_async_copy(query_gain, gains.at[0], loc_sem.at[7]),
        "key_gain": pltpu.make_async_copy(key_gain, gains.at[1], loc_sem.at[8]),
        "gate": pltpu.make_async_copy(gate, gate_row, loc_sem.at[9]),
        "out_weight": pltpu.make_async_copy(
            out_weight.at[:, columns], wo.at[group], loc_sem.at[10]
        ),
    }
    local[WEIGHTS] = pltpu.make_async_copy(weight.at[:, :, here], wbuf.at[me], loc_sem.at[11])
    staged = {
        WEIGHTS: pltpu.make_async_copy(weight.at[:, :, there], stage, loc_sem.at[12]),
        KEYS: pltpu.make_async_copy(stale_keys.at[:, there], stage_kv.at[0], loc_sem.at[13]),
        VALUES: pltpu.make_async_copy(stale_values.at[:, there], stage_kv.at[1], loc_sem.at[14]),
    }
    for name in KINDS:
        local[name].start()
        staged[name].start()
    for name, copy in local.items():
        if name not in KINDS:
            copy.start()

    for copy in staged.values():
        copy.wait()
    pl.semaphore_wait(barrier, len(everyone))

    def chunk(kind, stream, offset, core):
        side = yh if stream == 0 else 1 - yh
        index = lax.rem(z + offset + NZ, NZ) * 4 + side * 2 + core
        return wbuf.at[index] if kind == WEIGHTS else kv.at[index, KINDS.index(kind) - 1]

    def ring(kind, stream, way, step):
        ref = chunk(kind, stream, (1 - step) if way == 0 else (step - 1), c)
        at = (KINDS.index(kind) * 2 + stream) * 2 + way
        return COPY(
            ref, ref, ring_send.at[at, step], ring_recv.at[at, step],
            device_id=next_z if way == 0 else last_z, device_id_type=MESH,
        )

    def ring_arrival(kind, stream, way, step):
        ref = chunk(kind, stream, -step if way == 0 else step, c)
        at = (KINDS.index(kind) * 2 + stream) * 2 + way
        return COPY(
            ref, ref, ring_send.at[at, step], ring_recv.at[at, step],
            device_id=next_z if way == 0 else last_z, device_id_type=MESH,
        )

    def sibling(kind, stream, offset, core):
        side = yh if stream == 0 else 1 - yh
        slot = lax.rem(offset + NZ, NZ)
        index = lax.rem(z + slot, NZ) * 4 + side * 2 + core
        ref = wbuf.at[index] if kind == WEIGHTS else kv.at[index]
        at = (kind == VALUES) * 2 + stream
        return COPY(
            ref, ref, sib_send.at[at, slot], sib_recv.at[at, slot],
            device_id=other_core, device_id_type=MESH,
        )

    def swap_copy(src, dst, at):
        return COPY(
            src, dst, swap_send.at[at], swap_recv.at[at], device_id=swap, device_id_type=MESH
        )

    partner = z * 4 + (1 - yh) * 2 + c
    swaps = [
        swap_copy(stage, wbuf.at[me], 0),
        swap_copy(stage_kv.at[0], kv.at[me, 0], 1),
        swap_copy(stage_kv.at[1], kv.at[me, 1], 2),
    ]
    swap_arrivals = [
        swap_copy(wbuf.at[partner], wbuf.at[partner], 0),
        swap_copy(kv.at[partner, 0], kv.at[partner, 0], 1),
        swap_copy(kv.at[partner, 1], kv.at[partner, 1], 2),
    ]

    def hid_copy(at, dx, dl, dh):
        return COPY(
            hidden, hid.at[yh, group], hid_send.at[at], hid_recv.at[at],
            device_id=plane_peer(dx, dl, dh), device_id_type=MESH,
        )

    def source_group(dx, dl):
        return lax.rem(x + 4 - dx, 4) * 2 + lax.rem(yl + dl, 2)

    def hid_arrival(at, dx, dl, dh):
        slot = hid.at[lax.rem(yh + dh, 2), source_group(dx, dl)]
        return COPY(
            slot, slot, hid_send.at[at], hid_recv.at[at],
            device_id=plane_peer(dx, dl, dh), device_id_type=MESH,
        )

    half = pl.ds(pl.multiple_of(c * 128, 128), 128)
    other_half = pl.ds(pl.multiple_of((1 - c) * 128, 128), 128)

    def wo_copy(at, dx, dl):
        peer = plane_peer(dx, dl, 0)
        src = out_weight.at[half, pl.ds(pl.multiple_of(peer[1] * 384, 384), 384)]
        return COPY(
            src, wo.at[group, half], wo_send.at[at], wo_recv.at[at],
            device_id=peer, device_id_type=MESH,
        )

    def wo_arrival(at, dx, dl):
        slot = wo.at[source_group(dx, dl), half]
        return COPY(
            slot, slot, wo_send.at[at], wo_recv.at[at],
            device_id=plane_peer(dx, dl, 0), device_id_type=MESH,
        )

    def wo_share(at, dx, dl, rows):
        slot = wo.at[source_group(dx, dl), rows]
        return COPY(
            slot, slot, wos_send.at[at], wos_recv.at[at],
            device_id=other_core, device_id_type=MESH,
        )

    def forward(kind, stream, step):
        if kind == WEIGHTS and step > 0:
            for offset in {1 - step, step - 1}:
                sibling(kind, stream, offset, 1 - c).wait_recv()
        if step == 0:
            (swap_arrivals[KINDS.index(kind)].wait_recv if stream else local[kind].wait)()
            ring(kind, stream, 0, 1).start()
            ring(kind, stream, 1, 1).start()
            if kind != KEYS:
                sibling(kind, stream, 0, c).start()
            return
        ways = [way for way in (0, 1) if step < 8 or stream == way]
        for way in ways:
            ring_arrival(kind, stream, way, step).wait_recv()
            if step < 7 or step == 7 and stream == way:
                ring(kind, stream, way, step + 1).start()
        for way in ways if kind != KEYS else ():
            sibling(kind, stream, -step if way == 0 else step, c).start()

    def norm(part):
        side, begin = part // 2, part % 2 * 4

        @pl.loop(begin, begin + 4, unroll=2)
        def _(block):
            rows = pl.ds(pl.multiple_of(block * 16, 16), 16)
            states = jnp.concatenate([hid[side, g, rows, :] for g in range(8)], axis=1)
            states = states.astype(F32)
            center = jnp.mean(states, axis=-1, keepdims=True)
            states = states - center
            spread = jnp.mean(states * states, axis=-1, keepdims=True)
            normed = states * lax.rsqrt(spread + 1e-06)
            modulated = (1.0 + scale_row[...]) * normed + shift_row[...]
            there = pl.ds(pl.multiple_of(side * 128 + block * 16, 16), 16)
            mod[there, :] = modulated.astype(BF16)

    def arrive_hidden():
        for name in ("hidden", "shift", "scale"):
            local[name].wait()
        for at, d in enumerate(PEERS):
            hid_arrival(at, *d).wait_recv()
        for at, d in enumerate(OUT_PEERS):
            wo_copy(at, *d).start()

    def project(pairs):
        for pair in pairs:
            at = lax.rem(z // 2 + pair + 8, 8)
            rows = [wbuf[pl.ds(at * 8, 8), part].reshape(384, 128) for part in range(3)]
            features = mod[:, pl.ds(pl.multiple_of(at * 384, 384), 384)]
            term = jnp.dot(features, jnp.concatenate(rows, axis=1), preferred_element_type=F32)
            proj[...] = term if pair == 0 else proj[...] + term

    def finish_projection():
        for stream in (0, 1):
            sibling(WEIGHTS, stream, 8, 1 - c).wait_recv()
        project((-3, 3, 4))
        for name in ("text_keys", "text_values", "query_gain", "key_gain"):
            local[name].wait()
        queries[...] = head_norm(proj[:, 0:128], gains[0])

    def head_norm(raw, gain):
        power = jnp.mean(raw * raw, axis=-1, keepdims=True)
        return (raw * lax.rsqrt(power + 1e-06) * gain).astype(BF16)


    def scores_of(rows, keys):
        return lax.dot_general(
            queries[rows, :], keys, (((1,), (1,)), ((), ())), preferred_element_type=F32
        )

    def lane_sums(exps):
        parts = [exps[:, i : i + 128] for i in range(0, exps.shape[1], 128)]
        return functools.reduce(lambda a, b: a + b, parts)

    def start_attend(rows, keys, values):
        scores = scores_of(rows, keys)
        top = jnp.max(scores, axis=-1, keepdims=True)
        exps = jnp.exp2((scores - top) * EXP_SCALE)
        peak[rows, :] = jnp.broadcast_to(top, (scores.shape[0], 128))
        total[rows, :] = lane_sums(exps)
        mixed[rows, :] = jnp.dot(exps.astype(BF16), values, preferred_element_type=F32)

    def attend(rows, keys, values):
        scores = scores_of(rows, keys)
        before = peak[rows, :]
        top = jnp.maximum(before, jnp.max(scores, axis=-1, keepdims=True))
        rescale = jnp.exp2((before - top) * EXP_SCALE)
        exps = jnp.exp2((scores - top[:, 0:1]) * EXP_SCALE)
        peak[rows, :] = top
        total[rows, :] = total[rows, :] * rescale + lane_sums(exps)
        mixed[rows, :] = mixed[rows, :] * rescale + jnp.dot(
            exps.astype(BF16), values, preferred_element_type=F32
        )

    every = pl.ds(0, 256)

    def siblings_of(offset):
        for stream in (0, 1):
            sibling(VALUES, stream, offset, 1 - c).wait_recv()

    def attend_own():
        start_attend(every, text[0], text[1])
        siblings_of(0)
        for side in (0, 1):
            rows = pl.ds(side * 128, 128)
            own_keys[...] = kv[pl.ds(z * 4, 4), 0]
            own_values[...] = kv[pl.ds(z * 4, 4), 1]
            own_keys[side * 2 + c] = head_norm(proj[rows, 128:256], gains[1])
            own_values[side * 2 + c] = proj[rows, 256:384].astype(BF16)
            attend(rows, own_keys[...].reshape(512, 128), own_values[...].reshape(512, 128))

    def plane(which, offset):
        return kv[pl.ds(lax.rem(z + offset, NZ) * 4, 4), which].reshape(512, 128)

    def attend_planes(offsets):
        for offset in offsets:
            siblings_of(offset)
        keys = jnp.concatenate([plane(0, offset) for offset in offsets], axis=0)
        values = jnp.concatenate([plane(1, offset) for offset in offsets], axis=0)
        attend(every, keys, values)

    def attend_pairs(first, count):
        @pl.loop(0, count // 2)
        def _(i):
            near = first + 2 * i
            attend_planes((near, NZ - near, near + 1, NZ - 1 - near))

    def attend_last():
        attend_planes((7, NZ - 7, 8))

    def share():
        for at, d in enumerate(OUT_PEERS):
            wo_arrival(at, *d).wait_recv()
            wo_share(at, *d, half).start()

    swaps[0].start()
    forward(WEIGHTS, 0, 0)
    swaps[1].start()
    swaps[2].start()
    forward(KEYS, 0, 0)
    forward(VALUES, 0, 0)

    hidden_due = list(enumerate(PEERS))
    for task, first, second in ORDER:
        if hidden_due:
            at, d = hidden_due.pop()
            hid_copy(at, *d).start()
        if task in KINDS:
            forward(task, first, second)
        elif task == "N":
            if first == 0:
                arrive_hidden()
            norm(first)
        elif task == "Q":
            project((0, -1, 1, -2, 2))
        elif task == "P":
            finish_projection()
        elif task == "O":
            attend_own()
        elif task == "S":
            share()
        elif task == "A":
            attend_pairs(first, second)
        else:
            attend_last()

    def attention(side):
        rows = pl.ds(side * 128, 128)
        sums = jnp.sum(total[rows, :], axis=-1, keepdims=True)
        return (mixed[rows, :] / sums).astype(BF16)

    def att_copy(at, dx, dl, dh):
        return COPY(
            mine.at[lax.rem(yh + dh, 2)], gathered.at[head], att_send.at[at], att_recv.at[at],
            device_id=plane_peer(dx, dl, dh), device_id_type=MESH,
        )

    def att_arrival(at, dx, dl, dh):
        slot = gathered.at[source_group(dx, dl) * 2 + lax.rem(yh + dh, 2)]
        return COPY(
            slot, slot, att_send.at[at], att_recv.at[at],
            device_id=plane_peer(dx, dl, dh), device_id_type=MESH,
        )

    def send_attention(dh):
        side = lax.rem(yh + dh, 2)
        mine[side] = attention(side)
        for at, d in reversed(list(enumerate(PEERS))):
            if d[2] == dh:
                att_copy(at, *d).start()

    send_attention(1)
    send_attention(0)

    for copy in swaps:
        copy.wait_send()
    for at, d in enumerate(PEERS):
        hid_copy(at, *d).wait_send()
    for at, d in enumerate(OUT_PEERS):
        wo_copy(at, *d).wait_send()
        wo_share(at, *d, half).wait_send()
    for kind in KINDS:
        for stream in (0, 1):
            for way in (0, 1):

                @pl.loop(1, 8)
                def _(step):
                    ring(kind, stream, way, step).wait_send()

            ring(kind, stream, stream, 8).wait_send()

            @pl.loop(0, NZ if kind != KEYS else 0)
            def _(slot):
                sibling(kind, stream, slot, c).wait_send()

    gathered[head] = mine[yh]
    local["out_weight"].wait()
    local["gate"].wait()
    for at, d in enumerate(OUT_PEERS):
        wo_share(at, *d, other_half).wait_recv()
    for at, d in enumerate(PEERS):
        att_arrival(at, *d).wait_recv()
    summed = jnp.zeros((128, 384), F32)
    for g in range(8):
        left = jnp.concatenate([gathered[2 * g], gathered[2 * g + 1]], axis=1)
        summed += jnp.dot(left, wo[g], preferred_element_type=F32)
    out[...] = (summed * gate_row[...].reshape(1, 384)).astype(BF16)

    for at, d in enumerate(PEERS):
        att_copy(at, *d).wait_send()


def per_device(
    hidden_states,
    shift_mod,
    scale_mod,
    gate_mod,
    qkv_weight,
    query_gain,
    key_gain,
    text_keys,
    text_values,
    stale_keys,
    stale_values,
    out_weight,
):
    dma = pltpu.SemaphoreType.DMA
    vmem = pl.BlockSpec(memory_space=pltpu.VMEM)
    hbm = pl.BlockSpec(memory_space=pltpu.HBM)
    n, m = len(PEERS), len(OUT_PEERS)
    return pl.pallas_call(
        kernel,
        name="joint_attention",
        out_shape=jax.ShapeDtypeStruct((128, 384), BF16),
        in_specs=[hbm] * 12,
        out_specs=vmem,
        scratch_shapes=[
            pltpu.VMEM((2, 8, 128, 384), BF16),
            pltpu.VMEM((256, 3072), BF16),
            pltpu.VMEM((3, 48, 128), BF16),
            pltpu.VMEM((2, 128, 128), BF16),
            pltpu.VMEM((64, 3, 48, 128), BF16),
            pltpu.VMEM((64, 2, 128, 128), BF16),
            pltpu.VMEM((1, 3072), F32),
            pltpu.VMEM((1, 3072), F32),
            pltpu.VMEM((384,), F32),
            pltpu.VMEM((2, 1, 128), F32),
            pltpu.VMEM((2, 512, 128), BF16),
            pltpu.VMEM((8, 256, 384), BF16),
            pltpu.VMEM((16, 128, 128), BF16),
            pltpu.VMEM((2, 128, 128), BF16),
            pltpu.VMEM((4, 128, 128), BF16),
            pltpu.VMEM((4, 128, 128), BF16),
            pltpu.VMEM((256, 384), F32),
            pltpu.VMEM((256, 128), BF16),
            pltpu.VMEM((256, 128), F32),
            pltpu.VMEM((256, 128), F32),
            pltpu.VMEM((256, 128), F32),
            dma((15,)),
            dma((5,)),
            dma((5,)),
            dma((12, 9)),
            dma((12, 9)),
            dma((4, NZ)),
            dma((4, NZ)),
            dma((n,)),
            dma((n,)),
            dma((m,)),
            dma((m,)),
            dma((m,)),
            dma((m,)),
            dma((n,)),
            dma((n,)),
        ],
        compiler_params=pltpu.CompilerParams(
            collective_id=0, has_side_effects=True, vmem_limit_bytes=60 * 1024 * 1024
        ),
        cost_estimate=pl.CostEstimate(
            flops=2_200_000_000, bytes_accessed=16_000_000, transcendentals=2_300_000
        ),
    )(
        hidden_states,
        shift_mod.reshape(1, -1),
        scale_mod.reshape(1, -1),
        gate_mod,
        qkv_weight.transpose(1, 0, 2),
        query_gain.reshape(1, -1),
        key_gain.reshape(1, -1),
        text_keys,
        text_values,
        stale_keys,
        stale_values,
        out_weight,
    )


def solution(mesh):
    placed = (
        P("patch", "head"),
        P(),
        P(),
        P("head"),
        P("patch", None, "head"),
        P(),
        P(),
        P(None, "head"),
        P(None, "head"),
        P("patch", "head"),
        P("patch", "head"),
        P("head", None),
    )
    return jax.shard_map(
        per_device, mesh=mesh, in_specs=placed, out_specs=P("patch", "head"), check_vma=False
    )
```

```python
import functools

import math

import jax
import jax.numpy as jnp
from jax import lax
from jax.experimental import pallas as pl
from jax.experimental.pallas import tpu as pltpu
from jax.sharding import PartitionSpec as P

MESH = pl.DeviceIdType.MESH
ORDER = (
    ("W", 0, 1), ("K", 0, 1), ("W", 1, 0), ("V", 0, 1), ("K", 1, 0), ("W", 0, 2), ("V", 1, 0), ("W", 1, 1),
    ("K", 0, 2), ("W", 0, 3), ("K", 1, 1), ("V", 1, 1), ("W", 1, 2), ("V", 0, 2), ("W", 0, 4), ("K", 1, 2),
    ("W", 1, 3), ("V", 1, 2), ("K", 0, 3), ("W", 0, 5), ("V", 0, 3), ("W", 1, 4), ("K", 1, 3), ("V", 1, 3),
    ("W", 0, 6), ("K", 0, 4), ("W", 1, 5), ("V", 0, 4), ("K", 1, 4), ("W", 0, 7), ("N", 0, 0), ("V", 1, 4),
    ("N", 1, 0), ("K", 0, 5), ("N", 2, 0), ("W", 1, 6), ("N", 3, 0), ("Q", 0, 0), ("V", 0, 5), ("W", 0, 8),
    ("K", 1, 5), ("V", 1, 5), ("K", 0, 6), ("W", 1, 7), ("V", 0, 6), ("K", 1, 6), ("V", 1, 6), ("K", 0, 7),
    ("W", 1, 8), ("V", 0, 7), ("P", 0, 0), ("K", 1, 7), ("V", 1, 7), ("O", 0, 0), ("K", 0, 8), ("A", 1, 2),
    ("S", 0, 0), ("V", 0, 8), ("K", 1, 8), ("V", 1, 8), ("A", 3, 4), ("L", 0, 0),
)
WEIGHTS, KEYS, VALUES = "WKV"
KINDS = (WEIGHTS, KEYS, VALUES)

NZ = 16
F32 = jnp.float32
BF16 = jnp.bfloat16
COPY = pltpu.make_async_remote_copy
EXP_SCALE = 128 ** (-0.5) * math.log2(math.e)
PEERS = [(dx, dl, dh) for dh in (0, 1) for dl in (0, 1) for dx in range(4)][1:]
OUT_PEERS = [(dx, dl) for dl in (0, 1) for dx in range(4)][1:]


def kernel(
    hidden,
    shift,
    scale,
    gate,
    weight,
    query_gain,
    key_gain,
    text_keys,
    text_values,
    stale_keys,
    stale_values,
    out_weight,
    out,
    hid,
    mod,
    stage,
    stage_kv,
    wbuf,
    kv,
    shift_row,
    scale_row,
    gate_row,
    gains,
    text,
    wo,
    gathered,
    mine,
    own_keys,
    own_values,
    proj,
    queries,
    peak,
    total,
    mixed,
    loc_sem,
    swap_send,
    swap_recv,
    ring_send,
    ring_recv,
    sib_send,
    sib_recv,
    hid_send,
    hid_recv,
    wo_send,
    wo_recv,
    wos_send,
    wos_recv,
    att_send,
    att_recv,
):
    me = lax.axis_index("patch")
    group = lax.axis_index("head")
    z, yh, c = me // 4, lax.rem(me // 2, 2), lax.rem(me, 2)
    x, yl = group // 2, lax.rem(group, 2)
    head = group * 2 + yh
    other_core = (z * 4 + yh * 2 + 1 - c, group)
    next_z = (lax.rem(z + 1, NZ) * 4 + yh * 2 + c, group)
    last_z = (lax.rem(z + NZ - 1, NZ) * 4 + yh * 2 + c, group)
    swap = (z * 4 + (1 - yh) * 2 + c, group)

    def plane_peer(dx, dl, dh):
        there = lax.rem(x + dx, 4) * 2 + lax.rem(yl + dl, 2)
        return (z * 4 + lax.rem(yh + dh, 2) * 2 + c, there)

    barrier = pltpu.get_barrier_semaphore()
    everyone = [plane_peer(*d) for d in PEERS[::-1]] + [next_z, last_z, other_core]
    for peer in everyone:
        pl.semaphore_signal(barrier, inc=1, device_id=peer, device_id_type=MESH)

    here = pl.ds(pl.multiple_of(yh * 128, 128), 128)
    there = pl.ds(pl.multiple_of((1 - yh) * 128, 128), 128)
    columns = pl.ds(pl.multiple_of(group * 384, 384), 384)
    local = {
        KEYS: pltpu.make_async_copy(stale_keys.at[:, here], kv.at[me, 0], loc_sem.at[0]),
        VALUES: pltpu.make_async_copy(stale_values.at[:, here], kv.at[me, 1], loc_sem.at[1]),
        "hidden": pltpu.make_async_copy(hidden, hid.at[yh, group], loc_sem.at[2]),
        "shift": pltpu.make_async_copy(shift, shift_row, loc_sem.at[3]),
        "scale": pltpu.make_async_copy(scale, scale_row, loc_sem.at[4]),
        "text_keys": pltpu.make_async_copy(text_keys.at[:, here], text.at[0], loc_sem.at[5]),
        "text_values": pltpu.make_async_copy(text_values.at[:, here], text.at[1], loc_sem.at[6]),
        "query_gain": pltpu.make_async_copy(query_gain, gains.at[0], loc_sem.at[7]),
        "key_gain": pltpu.make_async_copy(key_gain, gains.at[1], loc_sem.at[8]),
        "gate": pltpu.make_async_copy(gate, gate_row, loc_sem.at[9]),
        "out_weight": pltpu.make_async_copy(
            out_weight.at[:, columns], wo.at[group], loc_sem.at[10]
        ),
    }
    local[WEIGHTS] = pltpu.make_async_copy(weight.at[:, :, here], wbuf.at[me], loc_sem.at[11])
    staged = {
        WEIGHTS: pltpu.make_async_copy(weight.at[:, :, there], stage, loc_sem.at[12]),
        KEYS: pltpu.make_async_copy(stale_keys.at[:, there], stage_kv.at[0], loc_sem.at[13]),
        VALUES: pltpu.make_async_copy(stale_values.at[:, there], stage_kv.at[1], loc_sem.at[14]),
    }
    for name in KINDS:
        local[name].start()
        staged[name].start()
    for name, copy in local.items():
        if name not in KINDS:
            copy.start()

    for copy in staged.values():
        copy.wait()
    pl.semaphore_wait(barrier, len(everyone))

    def chunk(kind, stream, offset, core):
        side = yh if stream == 0 else 1 - yh
        index = lax.rem(z + offset + NZ, NZ) * 4 + side * 2 + core
        return wbuf.at[index] if kind == WEIGHTS else kv.at[index, KINDS.index(kind) - 1]

    def ring(kind, stream, way, step):
        ref = chunk(kind, stream, (1 - step) if way == 0 else (step - 1), c)
        at = (KINDS.index(kind) * 2 + stream) * 2 + way
        return COPY(
            ref, ref, ring_send.at[at, step], ring_recv.at[at, step],
            device_id=next_z if way == 0 else last_z, device_id_type=MESH,
        )

    def ring_arrival(kind, stream, way, step):
        ref = chunk(kind, stream, -step if way == 0 else step, c)
        at = (KINDS.index(kind) * 2 + stream) * 2 + way
        return COPY(
            ref, ref, ring_send.at[at, step], ring_recv.at[at, step],
            device_id=next_z if way == 0 else last_z, device_id_type=MESH,
        )

    def sibling(kind, stream, offset, core):
        side = yh if stream == 0 else 1 - yh
        slot = lax.rem(offset + NZ, NZ)
        index = lax.rem(z + slot, NZ) * 4 + side * 2 + core
        ref = wbuf.at[index] if kind == WEIGHTS else kv.at[index]
        at = (kind == VALUES) * 2 + stream
        return COPY(
            ref, ref, sib_send.at[at, slot], sib_recv.at[at, slot],
            device_id=other_core, device_id_type=MESH,
        )

    def swap_copy(src, dst, at):
        return COPY(
            src, dst, swap_send.at[at], swap_recv.at[at], device_id=swap, device_id_type=MESH
        )

    partner = z * 4 + (1 - yh) * 2 + c
    swaps = [
        swap_copy(stage, wbuf.at[me], 0),
        swap_copy(stage_kv.at[0], kv.at[me, 0], 1),
        swap_copy(stage_kv.at[1], kv.at[me, 1], 2),
    ]
    swap_arrivals = [
        swap_copy(wbuf.at[partner], wbuf.at[partner], 0),
        swap_copy(kv.at[partner, 0], kv.at[partner, 0], 1),
        swap_copy(kv.at[partner, 1], kv.at[partner, 1], 2),
    ]

    def hid_copy(at, dx, dl, dh):
        return COPY(
            hidden, hid.at[yh, group], hid_send.at[at], hid_recv.at[at],
            device_id=plane_peer(dx, dl, dh), device_id_type=MESH,
        )

    def source_group(dx, dl):
        return lax.rem(x + 4 - dx, 4) * 2 + lax.rem(yl + dl, 2)

    def hid_arrival(at, dx, dl, dh):
        slot = hid.at[lax.rem(yh + dh, 2), source_group(dx, dl)]
        return COPY(
            slot, slot, hid_send.at[at], hid_recv.at[at],
            device_id=plane_peer(dx, dl, dh), device_id_type=MESH,
        )

    half = pl.ds(pl.multiple_of(c * 128, 128), 128)
    other_half = pl.ds(pl.multiple_of((1 - c) * 128, 128), 128)

    def wo_copy(at, dx, dl):
        peer = plane_peer(dx, dl, 0)
        src = out_weight.at[half, pl.ds(pl.multiple_of(peer[1] * 384, 384), 384)]
        return COPY(
            src, wo.at[group, half], wo_send.at[at], wo_recv.at[at],
            device_id=peer, device_id_type=MESH,
        )

    def wo_arrival(at, dx, dl):
        slot = wo.at[source_group(dx, dl), half]
        return COPY(
            slot, slot, wo_send.at[at], wo_recv.at[at],
            device_id=plane_peer(dx, dl, 0), device_id_type=MESH,
        )

    def wo_share(at, dx, dl, rows):
        slot = wo.at[source_group(dx, dl), rows]
        return COPY(
            slot, slot, wos_send.at[at], wos_recv.at[at],
            device_id=other_core, device_id_type=MESH,
        )

    def forward(kind, stream, step):
        if kind == WEIGHTS and step > 0:
            for offset in {1 - step, step - 1}:
                sibling(kind, stream, offset, 1 - c).wait_recv()
        if step == 0:
            (swap_arrivals[KINDS.index(kind)].wait_recv if stream else local[kind].wait)()
            ring(kind, stream, 0, 1).start()
            ring(kind, stream, 1, 1).start()
            if kind != KEYS:
                sibling(kind, stream, 0, c).start()
            return
        ways = [way for way in (0, 1) if step < 8 or stream == way]
        for way in ways:
            ring_arrival(kind, stream, way, step).wait_recv()
            if step < 7 or step == 7 and stream == way:
                ring(kind, stream, way, step + 1).start()
        for way in ways if kind != KEYS else ():
            sibling(kind, stream, -step if way == 0 else step, c).start()

    def norm(part):
        side, begin = part // 2, part % 2 * 4

        @pl.loop(begin, begin + 4, unroll=2)
        def _(block):
            rows = pl.ds(pl.multiple_of(block * 16, 16), 16)
            states = jnp.concatenate([hid[side, g, rows, :] for g in range(8)], axis=1)
            states = states.astype(F32)
            center = jnp.mean(states, axis=-1, keepdims=True)
            states = states - center
            spread = jnp.mean(states * states, axis=-1, keepdims=True)
            normed = states * lax.rsqrt(spread + 1e-06)
            modulated = (1.0 + scale_row[...]) * normed + shift_row[...]
            there = pl.ds(pl.multiple_of(side * 128 + block * 16, 16), 16)
            mod[there, :] = modulated.astype(BF16)

    def arrive_hidden():
        for name in ("hidden", "shift", "scale"):
            local[name].wait()
        for at, d in enumerate(PEERS):
            hid_arrival(at, *d).wait_recv()
        for at, d in enumerate(OUT_PEERS):
            wo_copy(at, *d).start()

    def project(pairs):
        for pair in pairs:
            at = lax.rem(z // 2 + pair + 8, 8)
            rows = [wbuf[pl.ds(at * 8, 8), part].reshape(384, 128) for part in range(3)]
            features = mod[:, pl.ds(pl.multiple_of(at * 384, 384), 384)]
            term = jnp.dot(features, jnp.concatenate(rows, axis=1), preferred_element_type=F32)
            proj[...] = term if pair == 0 else proj[...] + term

    def finish_projection():
        for stream in (0, 1):
            sibling(WEIGHTS, stream, 8, 1 - c).wait_recv()
        project((-3, 3, 4))
        for name in ("text_keys", "text_values", "query_gain", "key_gain"):
            local[name].wait()
        queries[...] = head_norm(proj[:, 0:128], gains[0])

    def head_norm(raw, gain):
        power = jnp.mean(raw * raw, axis=-1, keepdims=True)
        return (raw * lax.rsqrt(power + 1e-06) * gain).astype(BF16)


    def scores_of(rows, keys):
        return lax.dot_general(
            queries[rows, :], keys, (((1,), (1,)), ((), ())), preferred_element_type=F32
        )

    def lane_sums(exps):
        parts = [exps[:, i : i + 128] for i in range(0, exps.shape[1], 128)]
        return functools.reduce(lambda a, b: a + b, parts)

    def start_attend(rows, keys, values):
        scores = scores_of(rows, keys)
        top = jnp.max(scores, axis=-1, keepdims=True)
        exps = jnp.exp2((scores - top) * EXP_SCALE)
        peak[rows, :] = jnp.broadcast_to(top, (scores.shape[0], 128))
        total[rows, :] = lane_sums(exps)
        mixed[rows, :] = jnp.dot(exps.astype(BF16), values, preferred_element_type=F32)

    def attend(rows, keys, values):
        scores = scores_of(rows, keys)
        before = peak[rows, :]
        top = jnp.maximum(before, jnp.max(scores, axis=-1, keepdims=True))
        rescale = jnp.exp2((before - top) * EXP_SCALE)
        exps = jnp.exp2((scores - top[:, 0:1]) * EXP_SCALE)
        peak[rows, :] = top
        total[rows, :] = total[rows, :] * rescale + lane_sums(exps)
        mixed[rows, :] = mixed[rows, :] * rescale + jnp.dot(
            exps.astype(BF16), values, preferred_element_type=F32
        )

    every = pl.ds(0, 256)

    def siblings_of(offset):
        for stream in (0, 1):
            sibling(VALUES, stream, offset, 1 - c).wait_recv()

    def attend_own():
        start_attend(every, text[0], text[1])
        siblings_of(0)
        for side in (0, 1):
            rows = pl.ds(side * 128, 128)
            own_keys[...] = kv[pl.ds(z * 4, 4), 0]
            own_values[...] = kv[pl.ds(z * 4, 4), 1]
            own_keys[side * 2 + c] = head_norm(proj[rows, 128:256], gains[1])
            own_values[side * 2 + c] = proj[rows, 256:384].astype(BF16)
            attend(rows, own_keys[...].reshape(512, 128), own_values[...].reshape(512, 128))

    def plane(which, offset):
        return kv[pl.ds(lax.rem(z + offset, NZ) * 4, 4), which].reshape(512, 128)

    def attend_planes(offsets):
        for offset in offsets:
            siblings_of(offset)
        keys = jnp.concatenate([plane(0, offset) for offset in offsets], axis=0)
        values = jnp.concatenate([plane(1, offset) for offset in offsets], axis=0)
        attend(every, keys, values)

    def attend_pairs(first, count):
        @pl.loop(0, count // 2)
        def _(i):
            near = first + 2 * i
            attend_planes((near, NZ - near, near + 1, NZ - 1 - near))

    def attend_last():
        attend_planes((7, NZ - 7, 8))

    def share():
        for at, d in enumerate(OUT_PEERS):
            wo_arrival(at, *d).wait_recv()
            wo_share(at, *d, half).start()

    swaps[0].start()
    forward(WEIGHTS, 0, 0)
    swaps[1].start()
    swaps[2].start()
    forward(KEYS, 0, 0)
    forward(VALUES, 0, 0)

    hidden_due = list(enumerate(PEERS))
    for task, first, second in ORDER:
        if hidden_due:
            at, d = hidden_due.pop()
            hid_copy(at, *d).start()
        if task in KINDS:
            forward(task, first, second)
        elif task == "N":
            if first == 0:
                arrive_hidden()
            norm(first)
        elif task == "Q":
            project((0, -1, 1, -2, 2))
        elif task == "P":
            finish_projection()
        elif task == "O":
            attend_own()
        elif task == "S":
            share()
        elif task == "A":
            attend_pairs(first, second)
        else:
            attend_last()

    def attention(side):
        rows = pl.ds(side * 128, 128)
        sums = jnp.sum(total[rows, :], axis=-1, keepdims=True)
        return (mixed[rows, :] / sums).astype(BF16)

    def att_copy(at, dx, dl, dh):
        return COPY(
            mine.at[lax.rem(yh + dh, 2)], gathered.at[head], att_send.at[at], att_recv.at[at],
            device_id=plane_peer(dx, dl, dh), device_id_type=MESH,
        )

    def att_arrival(at, dx, dl, dh):
        slot = gathered.at[source_group(dx, dl) * 2 + lax.rem(yh + dh, 2)]
        return COPY(
            slot, slot, att_send.at[at], att_recv.at[at],
            device_id=plane_peer(dx, dl, dh), device_id_type=MESH,
        )

    def send_attention(dh):
        side = lax.rem(yh + dh, 2)
        mine[side] = attention(side)
        for at, d in reversed(list(enumerate(PEERS))):
            if d[2] == dh:
                att_copy(at, *d).start()

    send_attention(1)
    send_attention(0)

    for copy in swaps:
        copy.wait_send()
    for at, d in enumerate(PEERS):
        hid_copy(at, *d).wait_send()
    for at, d in enumerate(OUT_PEERS):
        wo_copy(at, *d).wait_send()
        wo_share(at, *d, half).wait_send()
    for kind in KINDS:
        for stream in (0, 1):
            for way in (0, 1):

                @pl.loop(1, 8)
                def _(step):
                    ring(kind, stream, way, step).wait_send()

            ring(kind, stream, stream, 8).wait_send()

            @pl.loop(0, NZ if kind != KEYS else 0)
            def _(slot):
                sibling(kind, stream, slot, c).wait_send()

    gathered[head] = mine[yh]
    local["out_weight"].wait()
    local["gate"].wait()
    for at, d in enumerate(OUT_PEERS):
        wo_share(at, *d, other_half).wait_recv()
    summed = jnp.zeros((128, 384), F32)
    for dx, dl in ((0, 0), (1, 0), (3, 0), (0, 1), (1, 1), (3, 1), (2, 0), (2, 1)):
        for dh in (0, 1):
            if (dx, dl, dh) in PEERS:
                att_arrival(PEERS.index((dx, dl, dh)), dx, dl, dh).wait_recv()
        g = source_group(dx, dl)
        left = jnp.concatenate([gathered[2 * g], gathered[2 * g + 1]], axis=1)
        summed += jnp.dot(left, wo[g], preferred_element_type=F32)
    out[...] = (summed * gate_row[...].reshape(1, 384)).astype(BF16)

    for at, d in enumerate(PEERS):
        att_copy(at, *d).wait_send()


def per_device(
    hidden_states,
    shift_mod,
    scale_mod,
    gate_mod,
    qkv_weight,
    query_gain,
    key_gain,
    text_keys,
    text_values,
    stale_keys,
    stale_values,
    out_weight,
):
    dma = pltpu.SemaphoreType.DMA
    vmem = pl.BlockSpec(memory_space=pltpu.VMEM)
    hbm = pl.BlockSpec(memory_space=pltpu.HBM)
    n, m = len(PEERS), len(OUT_PEERS)
    return pl.pallas_call(
        kernel,
        name="joint_attention",
        out_shape=jax.ShapeDtypeStruct((128, 384), BF16),
        in_specs=[hbm] * 12,
        out_specs=vmem,
        scratch_shapes=[
            pltpu.VMEM((2, 8, 128, 384), BF16),
            pltpu.VMEM((256, 3072), BF16),
            pltpu.VMEM((3, 48, 128), BF16),
            pltpu.VMEM((2, 128, 128), BF16),
            pltpu.VMEM((64, 3, 48, 128), BF16),
            pltpu.VMEM((64, 2, 128, 128), BF16),
            pltpu.VMEM((1, 3072), F32),
            pltpu.VMEM((1, 3072), F32),
            pltpu.VMEM((384,), F32),
            pltpu.VMEM((2, 1, 128), F32),
            pltpu.VMEM((2, 512, 128), BF16),
            pltpu.VMEM((8, 256, 384), BF16),
            pltpu.VMEM((16, 128, 128), BF16),
            pltpu.VMEM((2, 128, 128), BF16),
            pltpu.VMEM((4, 128, 128), BF16),
            pltpu.VMEM((4, 128, 128), BF16),
            pltpu.VMEM((256, 384), F32),
            pltpu.VMEM((256, 128), BF16),
            pltpu.VMEM((256, 128), F32),
            pltpu.VMEM((256, 128), F32),
            pltpu.VMEM((256, 128), F32),
            dma((15,)),
            dma((5,)),
            dma((5,)),
            dma((12, 9)),
            dma((12, 9)),
            dma((4, NZ)),
            dma((4, NZ)),
            dma((n,)),
            dma((n,)),
            dma((m,)),
            dma((m,)),
            dma((m,)),
            dma((m,)),
            dma((n,)),
            dma((n,)),
        ],
        compiler_params=pltpu.CompilerParams(
            collective_id=0, has_side_effects=True, vmem_limit_bytes=60 * 1024 * 1024
        ),
        cost_estimate=pl.CostEstimate(
            flops=2_200_000_000, bytes_accessed=16_000_000, transcendentals=2_300_000
        ),
    )(
        hidden_states,
        shift_mod.reshape(1, -1),
        scale_mod.reshape(1, -1),
        gate_mod,
        qkv_weight.transpose(1, 0, 2),
        query_gain.reshape(1, -1),
        key_gain.reshape(1, -1),
        text_keys,
        text_values,
        stale_keys,
        stale_values,
        out_weight,
    )


def solution(mesh):
    placed = (
        P("patch", "head"),
        P(),
        P(),
        P("head"),
        P("patch", None, "head"),
        P(),
        P(),
        P(None, "head"),
        P(None, "head"),
        P("patch", "head"),
        P("patch", "head"),
        P("head", None),
    )
    return jax.shard_map(
        per_device, mesh=mesh, in_specs=placed, out_specs=P("patch", "head"), check_vma=False
    )
```
